256 devices in a mesh: row: 16 (over z, core), col: 8 (over y_hi, x), feat: 2 (over y_lo).
Axes of the slice: x: 4, y: 4 (y_hi: 2, y_lo: 2; y = y_hi * 2 + y_lo), z: 8, core: 2. Of those that a mesh axis runs over, the one named last changes fastest.
Arguments:
- node_feats: bfloat16 [32768, 512], P(('row', 'col'), 'feat'), may hold values from -6 to 6
- aggregated: bfloat16 [32768, 512], P(('row', 'col'), 'feat'), may hold values from -6 to 6
- cotangent: bfloat16 [32768, 512], P(('row', 'col'), 'feat'), may hold values from -6 to 6
- weight: bfloat16 [512, 512], P('feat'), may hold values from -0.25 to 0.25
- relation_vecs: bfloat16 [512, 512], P(None, 'feat'), may hold values from -6 to 6
- tile_vals: bfloat16 [16, 8, 384, 128, 128], P('row', 'col'), may hold values from -0.0390625 to 0.0390625
- tile_row: int32 [16, 8, 384], P('row', 'col'), may hold values from 0 to 15
- tile_col: int32 [16, 8, 384], P('row', 'col'), may hold values from 0 to 31
- tile_rel: int32 [16, 8, 384], P('row', 'col'), may hold values from 0 to 511
- tile_mask: int32 [16, 8, 384], P('row', 'col'), may hold values from 0 to 1, as said below
Outputs:
- node_grad: bfloat16 [32768, 512], P(('row', 'col'), 'feat')
- weight_grad: float32 [512, 512], P('feat')
- relation_grad: float32 [512, 512], P(None, 'feat')
The draws below stay inside these ranges and needn't reach their ends.
Inputs may be any that keep to these rules, and one draw needn't show every extreme that they name: On each device the live slots (tile_mask 1) come first in its list; some device has all 384 slots live; every device has at least one. Several tiles may share a block position.
All inputs are finite; a program needn't handle non-finite values.
Results may differ from the reference program's by a relative error of at most 0.0049.
Values may be sent and summed in bfloat16 or wider, within the bound.
A program may use at most 128 MiB of HBM per device.

```python
import math
import jax
import jax.numpy as jnp
from jax import lax

D = 512
NREL = 512
BLOCK = 128
NODE_DEV = 256
TILES_DEV = 384
BLOCKS_DEV = 2
NODES = 32768
N_ROW = 16
N_COL = 8


def layout(key):
    key_rows, key_cols, key_rels, key_shrink, key_fill = jax.random.split(key, 5)
    tile_shape = (N_ROW, N_COL, TILES_DEV)
    row_ids = jax.random.randint(key_rows, tile_shape, 0, N_COL * BLOCKS_DEV, dtype=jnp.int32)
    col_ids = jax.random.randint(key_cols, tile_shape, 0, N_ROW * BLOCKS_DEV, dtype=jnp.int32)
    rel_ids = jax.random.randint(key_rels, tile_shape, 0, NREL, dtype=jnp.int32)
    shrink = jax.random.randint(key_shrink, (N_ROW * N_COL,), 0, 4, dtype=jnp.int32)
    live_counts = TILES_DEV // jnp.left_shift(jnp.ones_like(shrink), shrink)
    filled = jax.random.randint(key_fill, (), 0, N_ROW * N_COL, dtype=jnp.int32)
    live_counts = jnp.where(jnp.arange(N_ROW * N_COL, dtype=jnp.int32) == filled, TILES_DEV, live_counts)
    mask_bits = (jnp.arange(TILES_DEV, dtype=jnp.int32)[None, :] < live_counts[:, None]).astype(jnp.int32)
    return (row_ids, col_ids, rel_ids, mask_bits.reshape(tile_shape))


def draw_tile_row(key, part):
    shared = layout(key)
    return shared[0]


def draw_tile_col(key, part):
    shared = layout(key)
    return shared[1]


def draw_tile_rel(key, part):
    shared = layout(key)
    return shared[2]


def draw_tile_mask(key, part):
    shared = layout(key)
    return shared[3]


def level_of(stream_key, shape, shards, least, top_value):
    factor_of = 1.0
    for position, blocks in shards:
        heights = jax.random.uniform(jax.random.fold_in(jax.random.fold_in(stream_key, 6), position), (blocks,), jnp.float32, least / len(shards), top_value / len(shards))
        factor_of = factor_of * jnp.repeat(jnp.exp(heights), shape[position] // blocks).reshape((-1,) + (1,) * (len(shape) - 1 - position))
    return factor_of


def noise(stream_key, shape, deviation, reach, cuts=(), kind=jnp.bfloat16):
    drawn = jax.random.normal(stream_key, shape, jnp.float32) * deviation
    if len(cuts) > 0:
        drawn = level_of(stream_key, shape, cuts, -0.22, 0.18) * drawn
    return jnp.clip(drawn, min=-reach, max=reach).astype(kind)


def setup_inputs(seed: int = 0) -> dict:
    keys = jax.random.split(jax.random.key(seed), 11)
    return {
        "node_feats": noise(keys[0], (NODES, D), 1.0, 6.0, ((0, 128), (1, 2))),
        "aggregated": noise(keys[1], (NODES, D), 1.0, 6.0, ((0, 128), (1, 2))),
        "cotangent": noise(keys[2], (NODES, D), 1.0, 6.0, ((0, 128), (1, 2))),
        "weight": noise(keys[3], (D, D), D ** -0.5, 0.25, ((0, 2),)),
        "relation_vecs": noise(keys[4], (NREL, D), 1.0, 6.0, ((1, 2),)),
        "tile_vals": noise(keys[5], (N_ROW, N_COL, TILES_DEV, BLOCK, BLOCK), (BLOCK * TILES_DEV // BLOCKS_DEV) ** -0.5, 0.0390625, ((0, 16), (1, 8))),
        "tile_row": draw_tile_row(jax.random.fold_in(keys[10], 71), 0),
        "tile_col": draw_tile_col(jax.random.fold_in(keys[10], 71), 0),
        "tile_rel": draw_tile_rel(jax.random.fold_in(keys[10], 71), 0),
        "tile_mask": draw_tile_mask(jax.random.fold_in(keys[10], 71), 0),
    }


def reference(node_feats, aggregated, cotangent, weight, relation_vecs, tile_vals, tile_row, tile_col, tile_rel, tile_mask):
    products = jnp.dot(cotangent, weight.T, preferred_element_type=jnp.float32).astype(jnp.bfloat16)
    weight_grad = jnp.dot(aggregated.T, cotangent, preferred_element_type=jnp.float32) * (NODES ** -0.5)
    width = node_feats.shape[1]
    row_panels = products.reshape(N_ROW, N_COL * BLOCKS_DEV, BLOCK, width)
    col_panels = node_feats.reshape(N_ROW, N_COL, BLOCKS_DEV, BLOCK, width)
    rel_table = relation_vecs.astype(jnp.float32)
    group_size = math.gcd(TILES_DEV, 64)

    def per_device(state, device_index):
        node_acc, rel_acc = state
        row_index = device_index // N_COL
        col_index = device_index % N_COL
        prod_panel = row_panels[row_index].astype(jnp.float32)
        feat_panel = col_panels[:, col_index].reshape(N_ROW * BLOCKS_DEV, BLOCK, width).astype(jnp.float32)
        tile_stack = tile_vals[row_index, col_index]
        row_list = tile_row[row_index, col_index].astype(jnp.int32)
        col_list = tile_col[row_index, col_index].astype(jnp.int32)
        rel_list = tile_rel[row_index, col_index].astype(jnp.int32)
        mask_list = tile_mask[row_index, col_index]

        def per_group(inner, group_index):
            col_acc, rel_part = inner
            first_slot = (group_index * group_size).astype(jnp.int32)
            blocks_here = lax.dynamic_slice_in_dim(tile_stack, first_slot, group_size, 0).astype(jnp.float32)
            row_ids = lax.dynamic_slice_in_dim(row_list, first_slot, group_size, 0)
            col_ids = lax.dynamic_slice_in_dim(col_list, first_slot, group_size, 0)
            rel_ids = lax.dynamic_slice_in_dim(rel_list, first_slot, group_size, 0)
            live_weight = lax.dynamic_slice_in_dim(mask_list, first_slot, group_size, 0).astype(jnp.float32)
            moved = jnp.einsum('kab,kad->kbd', blocks_here, prod_panel[row_ids], precision=lax.Precision.HIGHEST)
            scaled = moved * (rel_table[rel_ids] * live_weight[:, None])[:, None, :]
            col_acc = col_acc.at[col_ids].add(scaled)
            col_sums = jnp.sum(moved * feat_panel[col_ids], axis=1) * live_weight[:, None]
            rel_part = rel_part.at[rel_ids].add(col_sums)
            return (col_acc, rel_part), None

        start_state = (jnp.zeros((N_ROW * BLOCKS_DEV, BLOCK, width), jnp.float32), jnp.zeros((NREL, width), jnp.float32))
        (col_acc, rel_part), unused = lax.scan(per_group, start_state, jnp.arange(TILES_DEV // group_size, dtype=jnp.int32))
        node_acc = node_acc.at[:, col_index].add(col_acc.reshape(N_ROW, NODE_DEV, width))
        return (node_acc, rel_acc + rel_part), None

    start_all = (jnp.zeros((N_ROW, N_COL, NODE_DEV, width), jnp.float32), jnp.zeros((NREL, width), jnp.float32))
    (node_acc, relation_grad), unused = lax.scan(per_device, start_all, jnp.arange(N_ROW * N_COL, dtype=jnp.int32))
    node_grad = node_acc.reshape(NODES, width).astype(jnp.bfloat16)
    return (node_grad, weight_grad, relation_grad)
```

```python
import functools

import jax
import jax.numpy as jnp
from jax import lax
from jax.experimental import pallas as pl
from jax.experimental.pallas import tpu as pltpu
from jax.sharding import PartitionSpec as P

MESH = pl.DeviceIdType.MESH
BF16 = jnp.bfloat16
F32 = jnp.float32
NZ, NX, NY = 8, 4, 4


def place():
    row, col, feat = lax.axis_index("row"), lax.axis_index("col"), lax.axis_index("feat")
    return row // 2, row % 2, col % NX, (col // NX) * 2 + feat


def device_at(z, core, x, y):
    return {"row": z * 2 + core, "col": (y // 2) * NX + x, "feat": y % 2}


def greet(devices):
    barrier = pltpu.get_barrier_semaphore()
    for device in devices:
        pl.semaphore_signal(barrier, inc=1, device_id=device, device_id_type=MESH)
    pl.semaphore_wait(barrier, len(devices))


def dot(a, b, contract):
    return lax.dot_general(a, b, ((contract[0], contract[1]), ((), ())), preferred_element_type=F32)


def gather_kernel(
    feats, cot, agg, weight, p_out, f_out, w_out, cots, prods, send_sems, recv_sems, local_sems
):
    z, core, x, y = place()
    y_hi = y // 2
    z_next, z_prev = (z + 1) % NZ, (z + NZ - 1) % NZ
    x_next, x_prev = (x + 1) % NX, (x + NX - 1) % NX
    y_next, y_prev = (y + 1) % NY, (y + NY - 1) % NY
    to_z = (device_at(z_next, core, x, y), device_at(z_prev, core, x, y))
    to_x = (device_at(z, core, x_next, y), device_at(z, core, x_prev, y))
    to_y = (device_at(z, core, x, y_next), device_at(z, core, x, y_prev))
    sibling = device_at(z, 1 - core, x, y)
    halves = (pl.ds(0, 128), pl.ds(128, 128))
    pending = []

    def remote(i, src, dst, device, start=True):
        copy = pltpu.make_async_remote_copy(
            src_ref=src, dst_ref=dst, send_sem=send_sems.at[i], recv_sem=recv_sems.at[i],
            device_id=device, device_id_type=MESH,
        )
        if start:
            copy.start()
            pending.append(copy)
        return copy

    own_cot = pltpu.make_async_copy(cot, cots.at[y], local_sems.at[0])
    own_cot.start()
    own_feat = pltpu.make_async_copy(feats, f_out.at[2 * z + core], local_sems.at[1])
    own_feat.start()
    greet((*to_z, *to_x, *to_y, sibling))

    for side in range(2):
        remote(side, cot, cots.at[y], to_y[side])
    for side in range(2):
        remote(12 + side, feats, f_out.at[2 * z + core], to_z[side])
    remote(20, feats, f_out.at[2 * z + core], sibling)

    def arrived(i, ref, device):
        remote(i, ref, ref, device, start=False).wait_recv()

    y_from = (y_prev, y_next)
    z_from = [((z + NZ - s) % NZ, (z + s) % NZ) for s in range(5)]
    x_from = (x_prev, x_next)

    def pass_feats(step):
        for side in range(2):
            r = 2 * z_from[step][side] + core
            if step < 4:
                block = f_out.at[r]
                arrived(12 + 2 * (step - 1) + side, block, to_z[side])
                if step < 3:
                    remote(12 + 2 * step + side, block, block, to_z[side])
                else:
                    part = f_out.at[r, halves[side]]
                    remote(18 + side, part, part, to_z[side])
                remote(20 + 2 * step - 1 + side, block, block, sibling)
            else:
                part = f_out.at[r, halves[side]]
                arrived(18 + side, part, to_z[side])
                remote(27 + side, part, part, sibling)

    def make_products(hi, slot):
        total = dot(cots[2 * hi], weight[:, :256], ((1,), (1,)))
        total += dot(cots[2 * hi + 1], weight[:, 256:], ((1,), (1,)))
        prods[slot] = total.astype(BF16)
        keep = pltpu.make_async_copy(prods.at[slot], p_out.at[hi * NX + x], local_sems.at[2 + slot])
        keep.start()
        for side in range(2):
            remote(4 + 4 * slot + side, prods.at[slot], p_out.at[hi * NX + x], to_x[side])
        return keep

    def pass_products(hi, slot):
        for side in range(2):
            block = p_out.at[hi * NX + x_from[side]]
            arrived(4 + 4 * slot + side, block, to_x[side])
            part = p_out.at[hi * NX + x_from[side], halves[side]]
            remote(6 + 4 * slot + side, part, part, to_x[side])

    def last_products(hi, slot):
        for side in range(2):
            part = p_out.at[hi * NX + (x + 2) % NX, halves[side]]
            arrived(6 + 4 * slot + side, part, to_x[side])

    for side in range(2):
        arrived(side, cots.at[y_from[side]], to_y[side])
        part = cots.at[y_from[side], halves[side]]
        remote(2 + side, part, part, to_y[side])
    own_cot.wait()
    keep0 = make_products(y_hi, 0)
    pass_feats(1)
    for side in range(2):
        arrived(2 + side, cots.at[(y + 2) % NY, halves[side]], to_y[side])
    keep1 = make_products(1 - y_hi, 1)
    for half in range(2):
        w_out[256 * half : 256 * half + 256, :] = dot(agg[...], cots[2 * y_hi + half], ((0,), (0,)))
    pass_products(y_hi, 0)
    pass_feats(2)
    pass_products(1 - y_hi, 1)
    pass_feats(3)
    last_products(y_hi, 0)
    pass_feats(4)
    last_products(1 - y_hi, 1)

    own = 2 * z + (1 - core)
    arrived(20, f_out.at[own], sibling)
    for step in (1, 2, 3):
        for side in range(2):
            arrived(20 + 2 * step - 1 + side, f_out.at[2 * z_from[step][side] + 1 - core], sibling)
    for side in range(2):
        arrived(27 + side, f_out.at[2 * z_from[4][side] + 1 - core, halves[side]], sibling)
    own_feat.wait()
    keep0.wait()
    keep1.wait()
    for copy in pending:
        copy.wait_send()


def gather_call(feats, cot, agg, weight):
    any_spec = pl.BlockSpec(memory_space=pl.ANY)
    vmem = pl.BlockSpec(memory_space=pltpu.VMEM)
    return pl.pallas_call(
        gather_kernel,
        out_shape=(
            jax.ShapeDtypeStruct((8, 256, 256), BF16),
            jax.ShapeDtypeStruct((16, 256, 256), BF16),
            jax.ShapeDtypeStruct((512, 256), F32),
        ),
        in_specs=[any_spec, any_spec, vmem, vmem],
        out_specs=(any_spec, any_spec, vmem),
        scratch_shapes=[
            pltpu.VMEM((4, 256, 256), BF16),
            pltpu.VMEM((2, 256, 256), BF16),
            pltpu.SemaphoreType.DMA((29,)),
            pltpu.SemaphoreType.DMA((29,)),
            pltpu.SemaphoreType.DMA((4,)),
        ],
        compiler_params=pltpu.CompilerParams(
            collective_id=0, has_side_effects=True, vmem_limit_bytes=60 * 2**20
        ),
        name="gather_panels",
    )(feats, cot, agg, weight)


CHUNK = 48
GROUP = 16


def tile_kernel(
    row_h, col_h, rel_h, mask_h, vals_h, p_h, f_h, rv_h, col_out, rel_out,
    row_s, col_s, rel_s, mask_s, vals, p_v, f_v, rv_v, acc, rel_acc, f32, rv32, sems, val_sems,
):
    slots = vals.shape[0]
    chunks = slots // CHUNK
    small = [
        pltpu.make_async_copy(src, dst, sems.at[i])
        for i, (src, dst) in enumerate(
            ((row_h, row_s), (col_h, col_s), (rel_h, rel_s), (mask_h, mask_s), (p_h, p_v), (rv_h, rv_v), (f_h, f_v))
        )
    ]

    def chunk_copy(i):
        part = pl.ds(i * CHUNK, CHUNK)
        return pltpu.make_async_copy(vals_h.at[part], vals.at[part], val_sems.at[i])

    for copy in small:
        copy.start()
    for i in range(chunks):
        chunk_copy(i).start()

    @pl.loop(0, 32)
    def _(i):
        acc[i] = jnp.zeros((128, 256), F32)
        rel_acc[pl.ds(i * 16, 16)] = jnp.zeros((16, 8, 256), F32)

    for copy in small:
        copy.wait()
    rv32[...] = rv_v[...].astype(F32)

    @pl.loop(0, 32)
    def _(i):
        f32[i] = f_v[i].astype(F32)

    @pl.loop(0, chunks)
    def _(i):
        chunk_copy(i).wait()

        @pl.loop(0, CHUNK // GROUP)
        def _(j):
            base = i * CHUNK + j * GROUP

            @pl.when(mask_s[0, base] != 0)
            def _():
                for g in range(GROUP):
                    k = base + g
                    live = mask_s[0, k].astype(F32)
                    r, c, q = row_s[0, k], col_s[0, k], rel_s[0, k]
                    moved = dot(vals[k], p_v[r], ((0,), (0,)))
                    acc[c] += moved * (rv32[pl.ds(q, 1), :] * live)
                    rel_acc[q] += jnp.sum((moved * f32[c]).reshape(16, 8, 256), axis=0) * live

    @pl.loop(0, 32)
    def _(i):
        col_out[i] = acc[i].astype(BF16)

    rel_out[...] = jnp.sum(rel_acc[...], axis=1)


def tile_call(row, col, rel, mask, vals, p, f, rv):
    any_spec = pl.BlockSpec(memory_space=pl.ANY)
    vmem = pl.BlockSpec(memory_space=pltpu.VMEM)
    slots = vals.shape[0]
    return pl.pallas_call(
        tile_kernel,
        out_shape=(jax.ShapeDtypeStruct((32, 128, 256), BF16), jax.ShapeDtypeStruct((512, 256), F32)),
        in_specs=[any_spec] * 8,
        out_specs=(vmem, vmem),
        scratch_shapes=[
            *[pltpu.SMEM((1, slots), jnp.int32)] * 4,
            pltpu.VMEM((slots, 128, 128), BF16),
            pltpu.VMEM((16, 128, 256), BF16),
            pltpu.VMEM((32, 128, 256), BF16),
            pltpu.VMEM((512, 256), BF16),
            pltpu.VMEM((32, 128, 256), F32),
            pltpu.VMEM((512, 8, 256), F32),
            pltpu.VMEM((32, 128, 256), F32),
            pltpu.VMEM((512, 256), F32),
            pltpu.SemaphoreType.DMA((7,)),
            pltpu.SemaphoreType.DMA((slots // CHUNK,)),
        ],
        compiler_params=pltpu.CompilerParams(vmem_limit_bytes=60 * 2**20),
        name="tile_sums",
    )(row, col, rel, mask, vals, p, f, rv)


def reduce_kernel(
    scale, col_h, rel, w, node_out, w_out, rel_out,
    own, sib, tx, rx, xsib, y_f, y_b, rx_x, z_b, rx_y, v_f, rx_z, v_g, z_g, y_g, all_g,
    send_sems, recv_sems, local_sems,
):
    z, core, x, y = place()
    y_hi = y // 2
    other_y = (y + 2) % NY
    z_next, z_prev = (z + 1) % NZ, (z + NZ - 1) % NZ
    to_z = (device_at(z_next, core, x, y), device_at(z_prev, core, x, y))
    sibling = device_at(z, 1 - core, x, y)
    z_peers = [device_at((z + d) % NZ, core, x, y) for d in range(NZ)]
    x_peers = [device_at(z, core, (x + d) % NX, y) for d in range(NX)]
    y_peer = device_at(z, core, x, other_y)
    pending = []

    def remote(i, src, dst, device, start=True):
        copy = pltpu.make_async_remote_copy(
            src_ref=src, dst_ref=dst, send_sem=send_sems.at[i], recv_sem=recv_sems.at[i],
            device_id=device, device_id_type=MESH,
        )
        if start:
            copy.start()
            pending.append(copy)
        return copy

    def arrived(i, ref, device):
        remote(i, ref, ref, device, start=False).wait_recv()

    order = [(z + d) % NZ for d in (4, 3, 5, 2, 6, 1, 7, 0)]
    owns = [
        pltpu.make_async_copy(col_h.at[b, core], own.at[b], local_sems.at[i]) for i, b in enumerate(order)
    ]
    for copy in owns:
        copy.start()
    greet((sibling, y_peer, *z_peers[1:], *x_peers[1:]))

    theirs = pl.ds((1 - core) * 256, 256)
    mine = pl.ds(core * 256, 256)
    remote(0, rel.at[theirs], xsib.at[pl.ds(0, 256)], sibling)
    remote(1, w.at[theirs], xsib.at[pl.ds(256, 256)], sibling)
    for i, b in enumerate(order):
        remote(2 + i, col_h.at[b, 1 - core], sib.at[b], sibling)

    def block_sum(b, rows):
        return own[b, rows].astype(F32) + sib[b, rows].astype(F32)

    def block_ready(i):
        owns[i].wait()
        arrived(2 + i, sib.at[order[i]], sibling)

    halves = (pl.ds(0, 128), pl.ds(128, 128))

    def chain(side, step, half, i):
        rows = halves[half]
        total = block_sum(order[i], rows)
        if step >= 2 or (step == 1 and half == side):
            at = 10 + 8 * side + 2 * (step - 1) + half
            arrived(at, rx.at[side, step - 1, rows], to_z[side])
            total += rx[side, step - 1, rows].astype(F32)
        tx[side, step, rows] = total.astype(BF16)
        remote(
            10 + 8 * side + 2 * step + half, tx.at[side, step, rows], rx.at[side, step, rows], to_z[side]
        )

    arrived(0, xsib.at[pl.ds(0, 256)], sibling)
    arrived(1, xsib.at[pl.ds(256, 256)], sibling)
    y_f[0:256, :] = rel[mine, :] + xsib[0:256, :]
    y_f[256:512, :] = w[mine, :] + xsib[256:512, :]
    y_b[...] = y_f[...].astype(BF16)
    for d in (2, 1, 3):
        remote(25 + d, y_b.at[pl.ds(((x + d) % NX) * 128, 128)], rx_x.at[d], x_peers[d])
    block_ready(0)
    for side in range(2):
        chain(side, 0, side, 0)
    block_ready(1)
    chain(0, 1, 1, 1)
    block_ready(2)
    chain(1, 1, 0, 2)

    x_total = y_f[pl.ds(x * 128, 128), :]
    for d in (1, 3, 2):
        arrived(25 + d, rx_x.at[d], x_peers[d])
        x_total += rx_x[d].astype(F32)
    y_f[0:128, :] = x_total
    z_b[...] = x_total.astype(BF16)
    remote(29, z_b.at[pl.ds((1 - y_hi) * 64, 64)], rx_y, y_peer)

    chain(0, 1, 0, 1)
    chain(1, 1, 1, 2)
    block_ready(3)
    block_ready(4)
    for half in range(2):
        chain(0, 2, half, 3)
        chain(1, 2, half, 4)

    arrived(29, rx_y, y_peer)
    v_f[...] = (y_f[pl.ds(y_hi * 64, 64), :] + rx_y[...].astype(F32)).reshape(8, 8, 256)
    for d in (4, 3, 5, 2, 6, 1, 7):
        remote(29 + d, v_f.at[(z + d) % NZ], rx_z.at[d], z_peers[d])

    block_ready(5)
    block_ready(6)
    for half in range(2):
        chain(0, 3, half, 5)
        chain(1, 3, half, 6)

    z_total = v_f[z]
    for d in range(1, NZ):
        arrived(29 + d, rx_z.at[d], z_peers[d])
        z_total += rx_z[d]
    v_g[z] = z_total
    for d in (4, 3, 5, 2, 6, 1, 7):
        remote(36 + d, v_g.at[z], v_g.at[z], z_peers[d])
    for d in range(1, NZ):
        arrived(36 + d, v_g.at[(z + NZ - d) % NZ], z_peers[d])
    z_g[y_hi] = v_g[...].reshape(64, 256).astype(BF16)
    remote(44, z_g.at[y_hi], z_g.at[y_hi], y_peer)

    block_ready(7)
    node = [block_sum(z, halves[half]) for half in range(2)]
    for half in range(2):
        for side in range(2):
            arrived(16 + 8 * side + half, rx.at[side, 3, halves[half]], to_z[side])
        node_out[halves[half], :] = (
            node[half] + rx[0, 3, halves[half]].astype(F32) + rx[1, 3, halves[half]].astype(F32)
        ).astype(BF16)

    arrived(44, z_g.at[1 - y_hi], y_peer)
    y_g[x] = z_g[...].reshape(128, 256)
    for d in (2, 1, 3):
        remote(44 + d, y_g.at[x], y_g.at[x], x_peers[d])
    all_g[core, x] = y_g[x]
    remote(48, y_g.at[x], all_g.at[core, x], sibling)
    for d in (1, 3, 2):
        s = (x + NX - d) % NX
        arrived(44 + d, y_g.at[s], x_peers[d])
        remote(48 + d, y_g.at[s], all_g.at[core, s], sibling)
        all_g[core, s] = y_g[s]
    for d in range(NX):
        arrived(48 + d, all_g.at[1 - core, (x + NX - d) % NX], sibling)
    for k in range(2):
        for i in range(2):
            rel_out[256 * k + 128 * i : 256 * k + 128 * i + 128, :] = all_g[k, i].astype(F32)
            w_out[128 * i : 128 * i + 128, 256 * k : 256 * k + 256] = all_g[k, 2 + i].astype(F32) * scale
    for copy in pending:
        copy.wait_send()


def reduce_call(scale, cols, rel, w):
    any_spec = pl.BlockSpec(memory_space=pl.ANY)
    vmem = pl.BlockSpec(memory_space=pltpu.VMEM)
    return pl.pallas_call(
        functools.partial(reduce_kernel, scale),
        out_shape=(
            jax.ShapeDtypeStruct((256, 256), BF16),
            jax.ShapeDtypeStruct((256, 512), F32),
            jax.ShapeDtypeStruct((512, 256), F32),
        ),
        in_specs=[any_spec, vmem, vmem],
        out_specs=(vmem, vmem, vmem),
        scratch_shapes=[
            pltpu.VMEM((8, 256, 256), BF16),
            pltpu.VMEM((8, 256, 256), BF16),
            pltpu.VMEM((2, 4, 256, 256), BF16),
            pltpu.VMEM((2, 4, 256, 256), BF16),
            pltpu.VMEM((512, 256), F32),
            pltpu.VMEM((512, 256), F32),
            pltpu.VMEM((512, 256), BF16),
            pltpu.VMEM((4, 128, 256), BF16),
            pltpu.VMEM((128, 256), BF16),
            pltpu.VMEM((64, 256), BF16),
            pltpu.VMEM((8, 8, 256), F32),
            pltpu.VMEM((8, 8, 256), F32),
            pltpu.VMEM((8, 8, 256), F32),
            pltpu.VMEM((2, 64, 256), BF16),
            pltpu.VMEM((4, 128, 256), BF16),
            pltpu.VMEM((2, 4, 128, 256), BF16),
            pltpu.SemaphoreType.DMA((52,)),
            pltpu.SemaphoreType.DMA((52,)),
            pltpu.SemaphoreType.DMA((8,)),
        ],
        compiler_params=pltpu.CompilerParams(
            collective_id=1, has_side_effects=True, vmem_limit_bytes=60 * 2**20
        ),
        name="reduce_sums",
    )(cols, rel, w)


def on_device(
    node_feats, aggregated, cotangent, weight, relation_vecs, tile_vals, tile_row, tile_col, tile_rel, tile_mask
):
    nodes_total = node_feats.shape[0] * lax.axis_size("row") * lax.axis_size("col")
    slots, block = tile_vals.shape[2], tile_vals.shape[-1]
    p, f, w = gather_call(node_feats, cotangent, aggregated, weight)
    cols, rel = tile_call(
        tile_row.reshape(1, slots),
        tile_col.reshape(1, slots),
        tile_rel.reshape(1, slots),
        tile_mask.reshape(1, slots),
        tile_vals.reshape(slots, block, block),
        p.reshape(16, 128, 256),
        f.reshape(32, 128, 256),
        relation_vecs,
    )
    return reduce_call(nodes_total**-0.5, cols.reshape(8, 2, 256, 256), rel, w)


def solution(mesh):
    return jax.shard_map(
        on_device,
        mesh=mesh,
        in_specs=(
            P(("row", "col"), "feat"),
            P(("row", "col"), "feat"),
            P(("row", "col"), "feat"),
            P("feat", None),
            P(None, "feat"),
            P("row", "col", None, None, None),
            P("row", "col", None),
            P("row", "col", None),
            P("row", "col", None),
            P("row", "col", None),
        ),
        out_specs=(P(("row", "col"), "feat"), P("feat", None), P(None, "feat")),
        check_vma=False,
    )
```

```python
import functools

import jax
import jax.numpy as jnp
from jax import lax
from jax.experimental import pallas as pl
from jax.experimental.pallas import tpu as pltpu
from jax.sharding import PartitionSpec as P

MESH = pl.DeviceIdType.MESH
BF16 = jnp.bfloat16
F32 = jnp.float32
I32 = jnp.int32
NZ, NX, NY = 8, 4, 4
SLOTS = 384
GROUP = 16


def place():
    row, col, feat = lax.axis_index("row"), lax.axis_index("col"), lax.axis_index("feat")
    return row // 2, row % 2, col % NX, (col // NX) * 2 + feat


def device_at(z, core, x, y):
    return {"row": z * 2 + core, "col": (y // 2) * NX + x, "feat": y % 2}


def dot(a, b, contract):
    return lax.dot_general(a, b, ((contract[0], contract[1]), ((), ())), preferred_element_type=F32)


def columns_of(vector):
    return [
        jnp.transpose(jnp.broadcast_to(vector[:, 128 * b : 128 * b + 128], (128, 128))) for b in range(SLOTS // 128)
    ]


def over_rows(blocks):
    total = blocks[0]
    for block in blocks[1:]:
        total = total + block
    return jnp.sum(total, axis=0, keepdims=True)


def sort_tiles(row, col, rel, mask):
    slot = lax.broadcasted_iota(I32, (1, SLOTS), 1)
    key = col * 512 + slot + (1 - mask) * 32768
    packed = row + col * 16 + rel * 512 + slot * 262144
    key_columns = columns_of(key)
    lanes = lax.broadcasted_iota(I32, (128, 128), 1)
    ranks = [
        over_rows([(k < key[:, 128 * b : 128 * b + 128]).astype(I32) for k in key_columns])
        for b in range(SLOTS // 128)
    ]
    rank_columns = columns_of(jnp.concatenate(ranks, axis=1))
    packed_columns = columns_of(packed)
    ordered = [
        over_rows([jnp.where(r == lanes + 128 * b, p, 0) for r, p in zip(rank_columns, packed_columns)])
        for b in range(SLOTS // 128)
    ]
    counts = over_rows([(k < (lanes + 1) * 512).astype(I32) for k in key_columns])
    return jnp.concatenate(ordered, axis=1), counts


def layer_kernel(
    feats, cot, agg_h, weight_h, rv_h, vals_h, row_h, col_h, rel_h, mask_h,
    node_out, w_out, rel_out,
    lists, meta_v, meta_s, vals, panel, f_panel, f_wide, rv, rv_wide, agg, weight, cots,
    run, steps, parts, prefix, sums, sib,
    share, share_in, half_f, half_b, col_in, z_in, full,
    tx, rx, send_sems, recv_sems, local_sems,
):
    z, core, x, y = place()
    y_hi = y // 2
    c_me = y_hi * NX + x
    sibling = device_at(z, 1 - core, x, y)
    z_at = [(z + d) % NZ for d in range(NZ)]
    z_dev = [device_at(z_at[d], core, x, y) for d in range(NZ)]
    y_dev = [device_at(z, core, x, (y + d) % NY) for d in range(NY)]
    col_offsets = [(2, 2), (1, 2), (3, 2), (0, 2), (2, 0), (1, 0), (3, 0)]
    col_dev = [device_at(z, core, (x + dx) % NX, (y + dy) % NY) for dx, dy in col_offsets]
    col_to = [(((y + dy) % NY) // 2) * NX + (x + dx) % NX for dx, dy in col_offsets]
    col_from = [(((y + dy) % NY) // 2) * NX + (x + NX - dx) % NX for dx, dy in col_offsets]
    pending = []
    taken = [0]

    def reserve(n):
        taken[0] += n
        return taken[0] - n

    def remote(i, src, dst, device):
        copy = pltpu.make_async_remote_copy(
            src_ref=src, dst_ref=dst, send_sem=send_sems.at[i], recv_sem=recv_sems.at[i],
            device_id=device, device_id_type=MESH,
        )
        copy.start()
        pending.append(copy)

    def arrived(i, ref, device):
        pltpu.make_async_remote_copy(
            src_ref=ref, dst_ref=ref, send_sem=send_sems.at[i], recv_sem=recv_sems.at[i],
            device_id=device, device_id_type=MESH,
        ).wait_recv()

    own_r = 2 * z + core
    local = [
        pltpu.make_async_copy(src, dst, local_sems.at[i])
        for i, (src, dst) in enumerate(
            (
                (row_h, lists.at[0]), (col_h, lists.at[1]), (rel_h, lists.at[2]), (mask_h, lists.at[3]),
                (cot, cots.at[y]), (weight_h, weight), (agg_h, agg), (feats, f_panel.at[own_r]),
                (rv_h, rv), (vals_h, vals),
            )
        )
    ]
    for copy in local:
        copy.start()

    barrier = pltpu.get_barrier_semaphore()
    greeted = [sibling, *z_dev[1:], *col_dev, y_dev[1], y_dev[3]]
    for device in greeted:
        pl.semaphore_signal(barrier, inc=1, device_id=device, device_id_type=MESH)
    for copy in local[:4]:
        copy.wait()
    mask = lists[3]
    ordered, counts = sort_tiles(lists[0], lists[1], lists[2], mask)
    meta_v[0:1, :] = ordered
    meta_v[1:2, 0:128] = counts
    meta_v[1:2, 128:384] = jnp.zeros((1, 256), I32)
    to_scalars = pltpu.make_async_copy(meta_v, meta_s, local_sems.at[10])
    to_scalars.start()
    pl.semaphore_wait(barrier, len(greeted))

    y_base, x_base, z_base, s_base = reserve(3), reserve(6), reserve(8), reserve(9)
    partner_side = (1, 3)
    for d in (1, 3, 2):
        remote(y_base + d - 1, cot, cots.at[y], y_dev[d])
    for j, d in enumerate((1, 7, 2, 6)):
        remote(z_base + j, feats, f_panel.at[own_r], z_dev[d])
    remote(s_base, feats, f_panel.at[own_r], sibling)

    def cot_arrived(d):
        arrived(y_base + d - 1, cots.at[(y + NY - d) % NY], y_dev[d])

    def f_slot(d, k):
        return 2 * ((z + NZ - d) % NZ) + k

    def make_products(hi, slot):
        total = dot(cots[2 * hi], weight[:, :256], ((1,), (1,)))
        total += dot(cots[2 * hi + 1], weight[:, 256:], ((1,), (1,)))
        panel[hi * NX + x] = total.astype(BF16).reshape(2, 128, 256)
        for j, d in enumerate((2, 1, 3)):
            remote(x_base + 3 * slot + j, panel.at[hi * NX + x], panel.at[hi * NX + x], device_at(z, core, (x + d) % NX, y))

    rv_wait = local[8]
    rv_wait.wait()
    rv_wide[...] = rv[...].astype(F32)
    run[...] = jnp.zeros_like(run)
    for copy in local[4:7]:
        copy.wait()
    cot_arrived(1)
    cot_arrived(3)
    make_products(y_hi, 0)

    ar_base = [reserve(1 + 7 + 7 + 7 + 8) for _ in range(2)]

    def share_send(a):
        remote(ar_base[a], share.at[a, pl.ds((1 - core) * 512, 512)], share_in.at[a], sibling)

    def share_cols(a):
        arrived(ar_base[a], share_in.at[a], sibling)
        total = share[a, pl.ds(core * 512, 512), :] + share_in[a]
        half_f[a] = total.reshape(8, 64, 128)
        half_b[a] = total.astype(BF16).reshape(8, 64, 128)
        for j in range(7):
            remote(ar_base[a] + 1 + j, half_b.at[a, col_to[j]], col_in.at[a, j], col_dev[j])

    def share_z(a):
        total = half_f[a, c_me]
        for j in range(7):
            arrived(ar_base[a] + 1 + j, col_in.at[a, j], col_dev[j])
            total += col_in[a, j].astype(F32)
        z_in[a, z] = total.astype(BF16)
        for d in (4, 3, 5, 2, 6, 1, 7):
            remote(ar_base[a] + 7 + d, z_in.at[a, z], z_in.at[a, z], z_dev[d])

    def share_back(a):
        for d in range(1, NZ):
            arrived(ar_base[a] + 7 + d, z_in.at[a, (z + NZ - d) % NZ], z_dev[d])
        total = z_in[a, 0].astype(F32)
        for d in range(1, NZ):
            total += z_in[a, d].astype(F32)
        mine = full.at[a, core, c_me]
        full[a, core, c_me] = total.astype(BF16)
        for j in range(7):
            remote(ar_base[a] + 15 + j, mine, mine, col_dev[j])
        remote(ar_base[a] + 22, mine, mine, sibling)

    def share_pass(a):
        for j in (6, 5, 3, 4, 2, 1, 0):
            block = full.at[a, core, col_from[j]]
            arrived(ar_base[a] + 15 + j, block, col_dev[j])
            remote(ar_base[a] + 23 + j, block, block, sibling)

    def share_end(a):
        arrived(ar_base[a] + 22, full.at[a, 1 - core, c_me], sibling)
        for j in range(7):
            arrived(ar_base[a] + 23 + j, full.at[a, 1 - core, col_from[j]], sibling)

    for j in range(2):
        w_part = dot(agg[...], cots[2 * y_hi + j], ((0,), (0,)))
        for i in range(2):
            at = 256 * (2 * j + i)
            share[0, at : at + 256, :] = w_part[:, 128 * i : 128 * i + 128]
    share_send(0)

    def f_pass(j, d):
        block = f_panel.at[f_slot(d, core)]
        arrived(z_base + j, block, z_dev[d])
        remote(s_base + 1 + j, block, block, sibling)

    f_pass(0, 1)
    f_pass(1, 7)
    cot_arrived(2)
    make_products(1 - y_hi, 1)
    share_cols(0)
    for side, d in enumerate((2, 6)):
        f_pass(2 + side, d)
        block = f_panel.at[f_slot(d, core)]
        remote(z_base + 4 + side, block, block, z_dev[(1, 7)[side]])
        part = f_panel.at[f_slot(d, core), side]
        remote(z_base + 6 + side, part, part, z_dev[d])
    f_pass(4, 3)
    f_pass(5, 5)
    for side in range(2):
        part = f_panel.at[f_slot(4, core), side]
        arrived(z_base + 6 + side, part, z_dev[4])
        remote(s_base + 7 + side, part, part, sibling)
    share_z(0)
    for slot, hi in enumerate((y_hi, 1 - y_hi)):
        for j, d in enumerate((2, 1, 3)):
            arrived(
                x_base + 3 * slot + j, panel.at[hi * NX + (x + NX - d) % NX], device_at(z, core, (x + d) % NX, y)
            )
    arrived(s_base, f_panel.at[2 * z + 1 - core], sibling)
    for j, d in enumerate((1, 7, 2, 6, 3, 5)):
        arrived(s_base + 1 + j, f_panel.at[f_slot(d, 1 - core)], sibling)
    for side in range(2):
        arrived(s_base + 7 + side, f_panel.at[f_slot(4, 1 - core), side], sibling)
    share_back(0)
    local[7].wait()
    local[9].wait()
    to_scalars.wait()

    @pl.loop(0, 16)
    def _(i):
        f_wide[i] = f_panel[i].astype(F32)

    @pl.loop(0, SLOTS // GROUP)
    def _(i):
        total = run[...]
        before = (meta_s[0, jnp.maximum(i * GROUP - 1, 0)] // 16) % 32
        for g in range(GROUP):
            at = i * GROUP + g
            code = meta_s[0, at]
            r, c, q, k = code % 16, (code // 16) % 32, (code // 512) % 512, code // 262144
            moved = dot(vals[k], panel[r // 2, r % 2], ((0,), (0,)))
            keep = (c == before).astype(F32)
            total = total * keep + moved * rv_wide[pl.ds(q, 1), :]
            prefix[at] = total.astype(BF16)
            parts[at] = jnp.sum((moved * f_wide[c // 2, c % 2]).reshape(16, 8, 256), axis=0)
            before = c
        run[...] = total

    rel_sorted = (meta_v[0:1, :] // 512) % 512
    live = lax.broadcasted_iota(I32, (1, SLOTS), 1) < jnp.sum(mask, axis=1, keepdims=True)
    pick = jnp.where(
        (lax.broadcasted_iota(I32, (512, SLOTS), 0) == rel_sorted) & live, 1.0, 0.0
    ).astype(BF16)
    tile_rows = jnp.sum(parts[...], axis=1)
    high = tile_rows.astype(BF16)
    low = (tile_rows - high.astype(F32)).astype(BF16)
    rel_part = dot(pick, high, ((1,), (0,))) + dot(pick, low, ((1,), (0,)))
    share[1, 0:512, :] = rel_part[:, :128]
    share[1, 512:1024, :] = rel_part[:, 128:]
    share_send(1)

    n_base, m_base = reserve(8), reserve(12)
    needed = (4, 3, 5, 1, 7, 2, 6, 0)

    def column_sum(j):
        count = meta_s[1, j]
        before = meta_s[1, jnp.maximum(j - 1, 0)] * (j > 0).astype(I32)
        some = (count > before).astype(F32)
        return (prefix[jnp.maximum(count - 1, 0)].astype(F32) * some).astype(BF16)

    for i, d in enumerate(needed):
        for h in range(2):
            sums[i, h] = column_sum(4 * z_at[d] + 2 * (1 - core) + h)
        remote(n_base + i, sums.at[i], sib.at[i], sibling)

    def both(i, h):
        return column_sum(4 * z_at[needed[i]] + 2 * core + h).astype(F32) + sib[i, h].astype(F32)

    def ready(i):
        arrived(n_base + i, sib.at[i], sibling)

    share_cols(1)
    ready(0)
    for side in range(2):
        tx[side, 0, side] = both(0, side).astype(BF16)
        remote(m_base + 6 * side, tx.at[side, 0, side], rx.at[side, 0, side], z_dev[(2, 6)[side]])
    for side in range(2):
        ready(1 + side)
        for h in (1 - side, side):
            tx[side, 1, h] = both(1 + side, h).astype(BF16)
            remote(m_base + 6 * side + 1 + h, tx.at[side, 1, h], rx.at[side, 1, h], z_dev[(1, 7)[side]])
    share_z(1)
    for side in range(2):
        ready(3 + side)
        for h in range(2):
            tx[side, 2, h] = both(3 + side, h).astype(BF16)
        remote(m_base + 6 * side + 3, tx.at[side, 2], rx.at[side, 2], z_dev[(1, 7)[side]])
    for side in range(2):
        ready(5 + side)
    for turn in range(2):
        for side in range(2):
            h = (1 - side, side)[turn]
            total = both(5 + side, h)
            arrived(m_base + 6 * side + 1 + h, rx.at[side, 1, h], z_dev[(1, 7)[side]])
            total += rx[side, 1, h].astype(F32)
            if turn == 1:
                arrived(m_base + 6 * side, rx.at[side, 0, h], z_dev[(2, 6)[side]])
                total += rx[side, 0, h].astype(F32)
            tx[side, 3, h] = total.astype(BF16)
            remote(m_base + 6 * side + 4 + h, tx.at[side, 3, h], rx.at[side, 3, h], z_dev[(2, 6)[side]])
    share_back(1)
    share_pass(0)
    share_end(0)
    w_out[...] = full[0].reshape(1024, 128)
    ready(7)
    for side in range(2):
        arrived(m_base + 6 * side + 3, rx.at[side, 2], z_dev[(1, 7)[side]])
    for h in range(2):
        total = both(7, h) + rx[0, 2, h].astype(F32) + rx[1, 2, h].astype(F32)
        for side in range(2):
            arrived(m_base + 6 * side + 4 + h, rx.at[side, 3, h], z_dev[(2, 6)[side]])
            total += rx[side, 3, h].astype(F32)
        node_out[128 * h : 128 * h + 128, :] = total.astype(BF16)
    share_pass(1)
    share_end(1)
    rel_out[...] = full[1].reshape(1024, 128)
    for copy in pending:
        copy.wait_send()


def layer_call(*operands):
    hbm = pl.BlockSpec(memory_space=pltpu.HBM)
    vmem = pl.BlockSpec(memory_space=pltpu.VMEM)
    return pl.pallas_call(
        layer_kernel,
        out_shape=(
            jax.ShapeDtypeStruct((256, 256), BF16),
            jax.ShapeDtypeStruct((1024, 128), BF16),
            jax.ShapeDtypeStruct((1024, 128), BF16),
        ),
        in_specs=[hbm] * 10,
        out_specs=(vmem, vmem, vmem),
        scratch_shapes=[
            pltpu.VMEM((4, 1, SLOTS), I32),
            pltpu.VMEM((2, SLOTS), I32),
            pltpu.SMEM((2, SLOTS), I32),
            pltpu.VMEM((SLOTS, 128, 128), BF16),
            pltpu.VMEM((8, 2, 128, 256), BF16),
            pltpu.VMEM((16, 2, 128, 256), BF16),
            pltpu.VMEM((16, 2, 128, 256), F32),
            pltpu.VMEM((512, 256), BF16),
            pltpu.VMEM((512, 256), F32),
            pltpu.VMEM((256, 256), BF16),
            pltpu.VMEM((256, 512), BF16),
            pltpu.VMEM((4, 256, 256), BF16),
            pltpu.VMEM((128, 256), F32),
            pltpu.VMEM((8, 128), F32),
            pltpu.VMEM((SLOTS, 8, 256), F32),
            pltpu.VMEM((SLOTS, 128, 256), BF16),
            pltpu.VMEM((8, 2, 128, 256), BF16),
            pltpu.VMEM((8, 2, 128, 256), BF16),
            pltpu.VMEM((2, 1024, 128), F32),
            pltpu.VMEM((2, 512, 128), F32),
            pltpu.VMEM((2, 8, 64, 128), F32),
            pltpu.VMEM((2, 8, 64, 128), BF16),
            pltpu.VMEM((2, 7, 64, 128), BF16),
            pltpu.VMEM((2, 8, 64, 128), BF16),
            pltpu.VMEM((2, 2, 8, 64, 128), BF16),
            pltpu.VMEM((2, 4, 2, 128, 256), BF16),
            pltpu.VMEM((2, 4, 2, 128, 256), BF16),
            pltpu.SemaphoreType.DMA((106,)),
            pltpu.SemaphoreType.DMA((106,)),
            pltpu.SemaphoreType.DMA((11,)),
        ],
        compiler_params=pltpu.CompilerParams(
            collective_id=0, has_side_effects=True, vmem_limit_bytes=62 * 2**20
        ),
        name="layer_backward",
    )(*operands)


def finish_kernel(scale, node, w, rel, node_out, w_out, rel_out):
    node_out[...] = node[...]
    for j in range(4):
        w_out[:, 128 * j : 128 * j + 128] = w[256 * j : 256 * j + 256, :].astype(F32) * scale
    for j in range(2):
        rel_out[:, 128 * j : 128 * j + 128] = rel[512 * j : 512 * j + 512, :].astype(F32)


def finish_call(scale, node, w, rel):
    vmem = pl.BlockSpec(memory_space=pltpu.VMEM)
    return pl.pallas_call(
        functools.partial(finish_kernel, scale),
        out_shape=(
            jax.ShapeDtypeStruct((256, 256), BF16),
            jax.ShapeDtypeStruct((256, 512), F32),
            jax.ShapeDtypeStruct((512, 256), F32),
        ),
        in_specs=[vmem] * 3,
        out_specs=(vmem,) * 3,
        name="finish",
    )(node, w, rel)


def on_device(
    node_feats, aggregated, cotangent, weight, relation_vecs, tile_vals, tile_row, tile_col, tile_rel, tile_mask
):
    nodes_total = node_feats.shape[0] * lax.axis_size("row") * lax.axis_size("col")
    node, w, rel = layer_call(
        node_feats.reshape(2, 128, 256),
        cotangent,
        aggregated,
        weight,
        relation_vecs,
        tile_vals.reshape(SLOTS, 128, 128),
        tile_row.reshape(1, SLOTS),
        tile_col.reshape(1, SLOTS),
        tile_rel.reshape(1, SLOTS),
        tile_mask.reshape(1, SLOTS),
    )
    return finish_call(nodes_total**-0.5, node, w, rel)


def solution(mesh):
    return jax.shard_map(
        on_device,
        mesh=mesh,
        in_specs=(
            P(("row", "col"), "feat"),
            P(("row", "col"), "feat"),
            P(("row", "col"), "feat"),
            P("feat", None),
            P(None, "feat"),
            P("row", "col", None, None, None),
            P("row", "col", None),
            P("row", "col", None),
            P("row", "col", None),
            P("row", "col", None),
        ),
        out_specs=(P(("row", "col"), "feat"), P("feat", None), P(None, "feat")),
        check_vma=False,
    )
```

```python
import functools

import jax
import jax.numpy as jnp
from jax import lax
from jax.experimental import pallas as pl
from jax.experimental.pallas import tpu as pltpu
from jax.sharding import PartitionSpec as P

MESH = pl.DeviceIdType.MESH
BF16 = jnp.bfloat16
F32 = jnp.float32
I32 = jnp.int32
NZ, NX, NY = 8, 4, 4
SLOTS = 384
GROUP = 32
PART = 96


def place():
    row, col, feat = lax.axis_index("row"), lax.axis_index("col"), lax.axis_index("feat")
    return row // 2, row % 2, col % NX, (col // NX) * 2 + feat


def device_at(z, core, x, y):
    return {"row": z * 2 + core, "col": (y // 2) * NX + x, "feat": y % 2}


def dot(a, b, contract):
    return lax.dot_general(a, b, ((contract[0], contract[1]), ((), ())), preferred_element_type=F32)


def columns_of(vector):
    return [
        jnp.transpose(jnp.broadcast_to(vector[:, 128 * b : 128 * b + 128], (128, 128))) for b in range(SLOTS // 128)
    ]


def over_rows(blocks):
    total = blocks[0]
    for block in blocks[1:]:
        total = total + block
    return jnp.sum(total, axis=0, keepdims=True)


def sort_tiles(row, col, rel, mask):
    slot = lax.broadcasted_iota(I32, (1, SLOTS), 1)
    key = col * 512 + slot + (1 - mask) * 32768
    packed = row + col * 16 + rel * 512 + slot * 262144
    key_columns = columns_of(key)
    lanes = lax.broadcasted_iota(I32, (128, 128), 1)
    ranks = [
        over_rows([(k < key[:, 128 * b : 128 * b + 128]).astype(I32) for k in key_columns])
        for b in range(SLOTS // 128)
    ]
    rank_columns = columns_of(jnp.concatenate(ranks, axis=1))
    packed_columns = columns_of(packed)
    ordered = [
        over_rows([jnp.where(r == lanes + 128 * b, p, 0) for r, p in zip(rank_columns, packed_columns)])
        for b in range(SLOTS // 128)
    ]
    counts = over_rows([(k < (lanes + 1) * 512).astype(I32) for k in key_columns])
    return jnp.concatenate(ordered, axis=1), counts


def layer_kernel(
    feats, cot, agg_h, weight_h, rv_h, vals_h, row_h, col_h, rel_h, mask_h,
    node_out, w_out, rel_out,
    lists, meta_v, meta_s, vals, panel, f_panel, f_wide, rv, rv_wide, agg, weight, cots,
    run, steps, parts, prefix, sums, sib,
    share, share_in, half_f, half_b, col_in, z_in, full,
    tx, rx, send_sems, recv_sems, local_sems,
):
    z, core, x, y = place()
    y_hi = y // 2
    c_me = y_hi * NX + x
    sibling = device_at(z, 1 - core, x, y)
    z_at = [(z + d) % NZ for d in range(NZ)]
    z_dev = [device_at(z_at[d], core, x, y) for d in range(NZ)]
    y_dev = [device_at(z, core, x, (y + d) % NY) for d in range(NY)]
    col_offsets = [(2, 2), (1, 2), (3, 2), (0, 2), (2, 0), (1, 0), (3, 0)]
    col_dev = [device_at(z, core, (x + dx) % NX, (y + dy) % NY) for dx, dy in col_offsets]
    col_to = [(((y + dy) % NY) // 2) * NX + (x + dx) % NX for dx, dy in col_offsets]
    col_from = [(((y + dy) % NY) // 2) * NX + (x + NX - dx) % NX for dx, dy in col_offsets]
    pending = []
    taken = [0]

    def reserve(n):
        taken[0] += n
        return taken[0] - n

    def remote(i, src, dst, device):
        copy = pltpu.make_async_remote_copy(
            src_ref=src, dst_ref=dst, send_sem=send_sems.at[i], recv_sem=recv_sems.at[i],
            device_id=device, device_id_type=MESH,
        )
        copy.start()
        pending.append(copy)

    def arrived(i, ref, device):
        pltpu.make_async_remote_copy(
            src_ref=ref, dst_ref=ref, send_sem=send_sems.at[i], recv_sem=recv_sems.at[i],
            device_id=device, device_id_type=MESH,
        ).wait_recv()

    own_r = 2 * z + core
    local = [
        pltpu.make_async_copy(src, dst, local_sems.at[i])
        for i, (src, dst) in enumerate(
            (
                (row_h, lists.at[0]), (col_h, lists.at[1]), (rel_h, lists.at[2]), (mask_h, lists.at[3]),
                (cot, cots.at[y]), (weight_h, weight), (agg_h, agg), (feats, f_panel.at[own_r]),
                (rv_h, rv),
                *((vals_h.at[pl.ds(PART * i, PART)], vals.at[pl.ds(PART * i, PART)]) for i in range(SLOTS // PART)),
            )
        )
    ]
    for copy in local:
        copy.start()

    barrier = pltpu.get_barrier_semaphore()
    greeted = [sibling, *z_dev[1:], *col_dev, y_dev[1], y_dev[3]]
    for device in greeted:
        pl.semaphore_signal(barrier, inc=1, device_id=device, device_id_type=MESH)
    run[...] = jnp.zeros_like(run)
    local[8].wait()
    rv_wide[...] = rv[...].astype(F32)

    def turn_tiles(i):
        local[9 + i].wait()

        @pl.loop(0, PART // 16)
        def _(j):
            for g in range(16):
                at = i * PART + j * 16 + g
                vals[at] = jnp.transpose(vals[at])

    pl.semaphore_wait(barrier, len(greeted))

    y_base, x_base, z_base, s_base = reserve(3), reserve(6), reserve(8), reserve(9)
    partner_side = (1, 3)
    for d in (1, 3, 2):
        remote(y_base + d - 1, cot, cots.at[y], y_dev[d])
    for j, d in enumerate((2, 6, 1, 7)):
        remote(z_base + j, feats, f_panel.at[own_r], z_dev[d])
    remote(s_base, feats, f_panel.at[own_r], sibling)

    for copy in local[:4]:
        copy.wait()
    mask = lists[3]
    ordered, counts = sort_tiles(lists[0], lists[1], lists[2], mask)
    meta_v[0:1, :] = ordered
    meta_v[1:2, 0:128] = counts
    meta_v[1:2, 128:384] = jnp.zeros((1, 256), I32)
    to_scalars = pltpu.make_async_copy(meta_v, meta_s, local_sems.at[13])
    to_scalars.start()

    def cot_arrived(d):
        arrived(y_base + d - 1, cots.at[(y + NY - d) % NY], y_dev[d])

    def f_slot(d, k):
        return 2 * ((z + NZ - d) % NZ) + k

    def make_products(hi, slot):
        total = dot(cots[2 * hi], weight[:, :256], ((1,), (1,)))
        total += dot(cots[2 * hi + 1], weight[:, 256:], ((1,), (1,)))
        panel[hi * NX + x] = total.astype(BF16).reshape(2, 128, 256)
        for j, d in enumerate((2, 1, 3)):
            remote(x_base + 3 * slot + j, panel.at[hi * NX + x], panel.at[hi * NX + x], device_at(z, core, (x + d) % NX, y))

    for copy in local[4:7]:
        copy.wait()
    cot_arrived(1)
    cot_arrived(3)
    make_products(y_hi, 0)

    ar_base = [reserve(1 + 7 + 7 + 7 + 8) for _ in range(2)]

    def share_send(a):
        remote(ar_base[a], share.at[a, pl.ds((1 - core) * 512, 512)], share_in.at[a], sibling)

    def share_cols(a):
        arrived(ar_base[a], share_in.at[a], sibling)
        total = share[a, pl.ds(core * 512, 512), :] + share_in[a]
        half_f[a] = total.reshape(8, 64, 128)
        half_b[a] = total.astype(BF16).reshape(8, 64, 128)
        for j in range(7):
            remote(ar_base[a] + 1 + j, half_b.at[a, col_to[j]], col_in.at[a, j], col_dev[j])

    def share_z(a):
        total = half_f[a, c_me]
        for j in range(7):
            arrived(ar_base[a] + 1 + j, col_in.at[a, j], col_dev[j])
            total += col_in[a, j].astype(F32)
        z_in[a, z] = total.astype(BF16)
        for d in (4, 3, 5, 2, 6, 1, 7):
            remote(ar_base[a] + 7 + d, z_in.at[a, z], z_in.at[a, z], z_dev[d])

    def share_back(a):
        for d in range(1, NZ):
            arrived(ar_base[a] + 7 + d, z_in.at[a, (z + NZ - d) % NZ], z_dev[d])
        total = z_in[a, 0].astype(F32)
        for d in range(1, NZ):
            total += z_in[a, d].astype(F32)
        mine = full.at[a, core, c_me]
        full[a, core, c_me] = total.astype(BF16)
        for j in range(7):
            remote(ar_base[a] + 15 + j, mine, mine, col_dev[j])
        remote(ar_base[a] + 22, mine, mine, sibling)

    def share_pass(a):
        for j in (6, 5, 3, 4, 2, 1, 0):
            block = full.at[a, core, col_from[j]]
            arrived(ar_base[a] + 15 + j, block, col_dev[j])
            remote(ar_base[a] + 23 + j, block, block, sibling)

    def share_end(a):
        arrived(ar_base[a] + 22, full.at[a, 1 - core, c_me], sibling)
        for j in range(7):
            arrived(ar_base[a] + 23 + j, full.at[a, 1 - core, col_from[j]], sibling)

    for j in range(2):
        w_part = dot(agg[...], cots[2 * y_hi + j], ((0,), (0,)))
        for i in range(2):
            at = 256 * (2 * j + i)
            share[0, at : at + 256, :] = w_part[:, 128 * i : 128 * i + 128]
    share_send(0)

    def f_pass(j, d):
        block = f_panel.at[f_slot(d, core)]
        arrived(z_base + j, block, z_dev[d])
        remote(s_base + 1 + j, block, block, sibling)

    turn_tiles(0)
    for side, d in enumerate((2, 6)):
        f_pass(side, d)
        block = f_panel.at[f_slot(d, core)]
        remote(z_base + 4 + side, block, block, z_dev[(1, 7)[side]])
        part = f_panel.at[f_slot(d, core), side]
        remote(z_base + 6 + side, part, part, z_dev[d])
    cot_arrived(2)
    make_products(1 - y_hi, 1)
    f_pass(2, 1)
    f_pass(3, 7)
    share_cols(0)
    for i in range(1, SLOTS // PART):
        turn_tiles(i)
    f_pass(4, 3)
    f_pass(5, 5)
    for side in range(2):
        part = f_panel.at[f_slot(4, core), side]
        arrived(z_base + 6 + side, part, z_dev[4])
        remote(s_base + 7 + side, part, part, sibling)
    for slot, hi in enumerate((y_hi, 1 - y_hi)):
        for j, d in enumerate((2, 1, 3)):
            arrived(
                x_base + 3 * slot + j, panel.at[hi * NX + (x + NX - d) % NX], device_at(z, core, (x + d) % NX, y)
            )
    arrived(s_base, f_panel.at[2 * z + 1 - core], sibling)
    for j, d in enumerate((2, 6, 1, 7, 3, 5)):
        arrived(s_base + 1 + j, f_panel.at[f_slot(d, 1 - core)], sibling)
    for side in range(2):
        arrived(s_base + 7 + side, f_panel.at[f_slot(4, 1 - core), side], sibling)
    share_z(0)
    local[7].wait()
    to_scalars.wait()

    @pl.loop(0, 16)
    def _(i):
        for h in range(2):
            f_wide[2 * i + h] = f_panel[i, h].astype(F32)

    @pl.loop(0, SLOTS // GROUP)
    def _(i):
        total = run[...]
        before = (meta_s[0, jnp.maximum(i * GROUP - 1, 0)] >> 4) & 31
        for g in range(GROUP):
            at = i * GROUP + g
            code = meta_s[0, at]
            r, c, q, k = code & 15, (code >> 4) & 31, (code >> 9) & 511, code >> 18
            moved = dot(vals[k], panel[r >> 1, r & 1], ((1,), (0,)))
            keep = (c == before).astype(F32)
            total = total * keep + moved * rv_wide[pl.ds(q, 1), :]
            prefix[at] = total.astype(BF16)
            parts[at] = jnp.sum((moved * f_wide[c]).reshape(16, 8, 256), axis=0)
            before = c
        run[...] = total

    n_base, m_base = reserve(8), reserve(12)
    needed = (4, 3, 5, 1, 7, 2, 6, 0)

    def column_sum(j):
        count = meta_s[1, j]
        before = meta_s[1, jnp.maximum(j - 1, 0)] * (j > 0).astype(I32)
        some = (count > before).astype(F32)
        return (prefix[jnp.maximum(count - 1, 0)].astype(F32) * some).astype(BF16)

    def send_sums(some):
        for i in some:
            for h in range(2):
                sums[i, h] = column_sum(4 * z_at[needed[i]] + 2 * (1 - core) + h)
            remote(n_base + i, sums.at[i], sib.at[i], sibling)

    send_sums(range(5))

    rel_sorted = (meta_v[0:1, :] // 512) % 512
    live = lax.broadcasted_iota(I32, (1, SLOTS), 1) < jnp.sum(mask, axis=1, keepdims=True)
    pick = jnp.where(
        (lax.broadcasted_iota(I32, (512, SLOTS), 0) == rel_sorted) & live, 1.0, 0.0
    ).astype(BF16)
    tile_rows = jnp.sum(parts[...], axis=1)
    high = tile_rows.astype(BF16)
    low = (tile_rows - high.astype(F32)).astype(BF16)
    rel_part = dot(pick, high, ((1,), (0,))) + dot(pick, low, ((1,), (0,)))
    share[1, 0:512, :] = rel_part[:, :128]
    share[1, 512:1024, :] = rel_part[:, 128:]
    share_send(1)
    send_sums(range(5, 8))

    def both(i, h):
        return column_sum(4 * z_at[needed[i]] + 2 * core + h).astype(F32) + sib[i, h].astype(F32)

    def ready(i):
        arrived(n_base + i, sib.at[i], sibling)

    ready(0)
    for side in range(2):
        tx[side, 0, side] = both(0, side).astype(BF16)
        remote(m_base + 6 * side, tx.at[side, 0, side], rx.at[side, 0, side], z_dev[(2, 6)[side]])
    for side in range(2):
        ready(1 + side)
        for h in (1 - side, side):
            tx[side, 1, h] = both(1 + side, h).astype(BF16)
            remote(m_base + 6 * side + 1 + h, tx.at[side, 1, h], rx.at[side, 1, h], z_dev[(1, 7)[side]])
    share_cols(1)
    for side in range(2):
        ready(3 + side)
        for h in range(2):
            tx[side, 2, h] = both(3 + side, h).astype(BF16)
        remote(m_base + 6 * side + 3, tx.at[side, 2], rx.at[side, 2], z_dev[(1, 7)[side]])
    share_back(0)
    share_z(1)
    for side in range(2):
        ready(5 + side)
    for turn in range(2):
        for side in range(2):
            h = (1 - side, side)[turn]
            total = both(5 + side, h)
            arrived(m_base + 6 * side + 1 + h, rx.at[side, 1, h], z_dev[(1, 7)[side]])
            total += rx[side, 1, h].astype(F32)
            if turn == 1:
                arrived(m_base + 6 * side, rx.at[side, 0, h], z_dev[(2, 6)[side]])
                total += rx[side, 0, h].astype(F32)
            tx[side, 3, h] = total.astype(BF16)
            remote(m_base + 6 * side + 4 + h, tx.at[side, 3, h], rx.at[side, 3, h], z_dev[(2, 6)[side]])
    share_pass(0)
    share_end(0)
    w_out[...] = full[0].reshape(1024, 128)
    share_back(1)
    ready(7)
    for side in range(2):
        arrived(m_base + 6 * side + 3, rx.at[side, 2], z_dev[(1, 7)[side]])
    for h in range(2):
        total = both(7, h) + rx[0, 2, h].astype(F32) + rx[1, 2, h].astype(F32)
        for side in range(2):
            arrived(m_base + 6 * side + 4 + h, rx.at[side, 3, h], z_dev[(2, 6)[side]])
            total += rx[side, 3, h].astype(F32)
        node_out[128 * h : 128 * h + 128, :] = total.astype(BF16)
    share_pass(1)
    share_end(1)
    rel_out[...] = full[1].reshape(1024, 128)
    for copy in pending:
        copy.wait_send()


def layer_call(*operands):
    hbm = pl.BlockSpec(memory_space=pltpu.HBM)
    vmem = pl.BlockSpec(memory_space=pltpu.VMEM)
    return pl.pallas_call(
        layer_kernel,
        out_shape=(
            jax.ShapeDtypeStruct((256, 256), BF16),
            jax.ShapeDtypeStruct((1024, 128), BF16),
            jax.ShapeDtypeStruct((1024, 128), BF16),
        ),
        in_specs=[hbm] * 10,
        out_specs=(vmem, vmem, vmem),
        scratch_shapes=[
            pltpu.VMEM((4, 1, SLOTS), I32),
            pltpu.VMEM((2, SLOTS), I32),
            pltpu.SMEM((2, SLOTS), I32),
            pltpu.VMEM((SLOTS, 128, 128), BF16),
            pltpu.VMEM((8, 2, 128, 256), BF16),
            pltpu.VMEM((16, 2, 128, 256), BF16),
            pltpu.VMEM((32, 128, 256), F32),
            pltpu.VMEM((512, 256), BF16),
            pltpu.VMEM((512, 256), F32),
            pltpu.VMEM((256, 256), BF16),
            pltpu.VMEM((256, 512), BF16),
            pltpu.VMEM((4, 256, 256), BF16),
            pltpu.VMEM((128, 256), F32),
            pltpu.VMEM((8, 128), F32),
            pltpu.VMEM((SLOTS, 8, 256), F32),
            pltpu.VMEM((SLOTS, 128, 256), BF16),
            pltpu.VMEM((8, 2, 128, 256), BF16),
            pltpu.VMEM((8, 2, 128, 256), BF16),
            pltpu.VMEM((2, 1024, 128), F32),
            pltpu.VMEM((2, 512, 128), F32),
            pltpu.VMEM((2, 8, 64, 128), F32),
            pltpu.VMEM((2, 8, 64, 128), BF16),
            pltpu.VMEM((2, 7, 64, 128), BF16),
            pltpu.VMEM((2, 8, 64, 128), BF16),
            pltpu.VMEM((2, 2, 8, 64, 128), BF16),
            pltpu.VMEM((2, 4, 2, 128, 256), BF16),
            pltpu.VMEM((2, 4, 2, 128, 256), BF16),
            pltpu.SemaphoreType.DMA((106,)),
            pltpu.SemaphoreType.DMA((106,)),
            pltpu.SemaphoreType.DMA((14,)),
        ],
        compiler_params=pltpu.CompilerParams(
            collective_id=0, has_side_effects=True, vmem_limit_bytes=62 * 2**20
        ),
        name="layer_backward",
    )(*operands)


def finish_kernel(scale, node, w, rel, node_out, w_out, rel_out):
    node_out[...] = node[...]
    for j in range(4):
        w_out[:, 128 * j : 128 * j + 128] = w[256 * j : 256 * j + 256, :].astype(F32) * scale
    for j in range(2):
        rel_out[:, 128 * j : 128 * j + 128] = rel[512 * j : 512 * j + 512, :].astype(F32)


def finish_call(scale, node, w, rel):
    vmem = pl.BlockSpec(memory_space=pltpu.VMEM)
    return pl.pallas_call(
        functools.partial(finish_kernel, scale),
        out_shape=(
            jax.ShapeDtypeStruct((256, 256), BF16),
            jax.ShapeDtypeStruct((256, 512), F32),
            jax.ShapeDtypeStruct((512, 256), F32),
        ),
        in_specs=[vmem] * 3,
        out_specs=(vmem,) * 3,
        name="finish",
    )(node, w, rel)


def on_device(
    node_feats, aggregated, cotangent, weight, relation_vecs, tile_vals, tile_row, tile_col, tile_rel, tile_mask
):
    nodes_total = node_feats.shape[0] * lax.axis_size("row") * lax.axis_size("col")
    node, w, rel = layer_call(
        node_feats.reshape(2, 128, 256),
        cotangent,
        aggregated,
        weight,
        relation_vecs,
        tile_vals.reshape(SLOTS, 128, 128),
        tile_row.reshape(1, SLOTS),
        tile_col.reshape(1, SLOTS),
        tile_rel.reshape(1, SLOTS),
        tile_mask.reshape(1, SLOTS),
    )
    return finish_call(nodes_total**-0.5, node, w, rel)


def solution(mesh):
    return jax.shard_map(
        on_device,
        mesh=mesh,
        in_specs=(
            P(("row", "col"), "feat"),
            P(("row", "col"), "feat"),
            P(("row", "col"), "feat"),
            P("feat", None),
            P(None, "feat"),
            P("row", "col", None, None, None),
            P("row", "col", None),
            P("row", "col", None),
            P("row", "col", None),
            P("row", "col", None),
        ),
        out_specs=(P(("row", "col"), "feat"), P("feat", None), P(None, "feat")),
        check_vma=False,
    )
```

```python
import functools

import jax
import jax.numpy as jnp
from jax import lax
from jax.experimental import pallas as pl
from jax.experimental.pallas import tpu as pltpu
from jax.sharding import PartitionSpec as P

MESH = pl.DeviceIdType.MESH
BF16 = jnp.bfloat16
F32 = jnp.float32
I32 = jnp.int32
NZ, NX, NY = 8, 4, 4
SLOTS = 384
GROUP = 48
PART = 96


def place():
    row, col, feat = lax.axis_index("row"), lax.axis_index("col"), lax.axis_index("feat")
    return row // 2, row % 2, col % NX, (col // NX) * 2 + feat


def device_at(z, core, x, y):
    return {"row": z * 2 + core, "col": (y // 2) * NX + x, "feat": y % 2}


def dot(a, b, contract):
    return lax.dot_general(a, b, ((contract[0], contract[1]), ((), ())), preferred_element_type=F32)


def columns_of(vector):
    return [
        jnp.transpose(jnp.broadcast_to(vector[:, 128 * b : 128 * b + 128], (128, 128))) for b in range(SLOTS // 128)
    ]


def over_rows(blocks):
    total = blocks[0]
    for block in blocks[1:]:
        total = total + block
    return jnp.sum(total, axis=0, keepdims=True)


def sort_tiles(row, col, rel, mask):
    slot = lax.broadcasted_iota(I32, (1, SLOTS), 1)
    key = col * 512 + slot + (1 - mask) * 32768
    packed = row + col * 16 + rel * 512 + slot * 262144
    key_columns = columns_of(key)
    lanes = lax.broadcasted_iota(I32, (128, 128), 1)
    ranks = [
        over_rows([(k < key[:, 128 * b : 128 * b + 128]).astype(I32) for k in key_columns])
        for b in range(SLOTS // 128)
    ]
    rank_columns = columns_of(jnp.concatenate(ranks, axis=1))
    packed_columns = columns_of(packed)
    ordered = [
        over_rows([jnp.where(r == lanes + 128 * b, p, 0) for r, p in zip(rank_columns, packed_columns)])
        for b in range(SLOTS // 128)
    ]
    counts = over_rows([(k < (lanes + 1) * 512).astype(I32) for k in key_columns])
    return jnp.concatenate(ordered, axis=1), counts


def layer_kernel(
    feats, cot, agg_h, weight_h, rv_h, vals_h, row_h, col_h, rel_h, mask_h,
    node_out, w_out, rel_out,
    lists, meta_v, meta_s, vals, panel, f_panel, f_wide, rv, rv_wide, agg, weight, cots,
    run, steps, parts, prefix, sums, sib,
    share, share_in, half_f, half_b, col_in, z_in, full,
    tx, rx, send_sems, recv_sems, local_sems,
):
    z, core, x, y = place()
    y_hi = y // 2
    c_me = y_hi * NX + x
    sibling = device_at(z, 1 - core, x, y)
    z_at = [(z + d) % NZ for d in range(NZ)]
    z_dev = [device_at(z_at[d], core, x, y) for d in range(NZ)]
    y_dev = [device_at(z, core, x, (y + d) % NY) for d in range(NY)]
    col_offsets = [(2, 2), (1, 2), (3, 2), (0, 2), (2, 0), (1, 0), (3, 0)]
    col_dev = [device_at(z, core, (x + dx) % NX, (y + dy) % NY) for dx, dy in col_offsets]
    col_to = [(((y + dy) % NY) // 2) * NX + (x + dx) % NX for dx, dy in col_offsets]
    col_from = [(((y + dy) % NY) // 2) * NX + (x + NX - dx) % NX for dx, dy in col_offsets]
    pending = []
    taken = [0]

    def reserve(n):
        taken[0] += n
        return taken[0] - n

    def remote(i, src, dst, device):
        copy = pltpu.make_async_remote_copy(
            src_ref=src, dst_ref=dst, send_sem=send_sems.at[i], recv_sem=recv_sems.at[i],
            device_id=device, device_id_type=MESH,
        )
        copy.start()
        pending.append(copy)

    def arrived(i, ref, device):
        pltpu.make_async_remote_copy(
            src_ref=ref, dst_ref=ref, send_sem=send_sems.at[i], recv_sem=recv_sems.at[i],
            device_id=device, device_id_type=MESH,
        ).wait_recv()

    own_r = 2 * z + core
    local = [
        pltpu.make_async_copy(src, dst, local_sems.at[i])
        for i, (src, dst) in enumerate(
            (
                (row_h, lists.at[0]), (col_h, lists.at[1]), (rel_h, lists.at[2]), (mask_h, lists.at[3]),
                (cot, cots.at[y]), (weight_h, weight), (agg_h, agg), (feats, f_panel.at[own_r]),
                (rv_h, rv),
                *((vals_h.at[pl.ds(PART * i, PART)], vals.at[pl.ds(PART * i, PART)]) for i in range(SLOTS // PART)),
            )
        )
    ]
    for copy in local:
        copy.start()

    barrier = pltpu.get_barrier_semaphore()
    greeted = [sibling, *z_dev[1:], *col_dev, y_dev[1], y_dev[3]]
    for device in greeted:
        pl.semaphore_signal(barrier, inc=1, device_id=device, device_id_type=MESH)
    run[...] = jnp.zeros_like(run)
    local[8].wait()
    rv_wide[...] = rv[...].astype(F32)

    def turn_tiles(i):
        local[9 + i].wait()

        @pl.loop(0, PART // 16)
        def _(j):
            for g in range(16):
                at = i * PART + j * 16 + g
                vals[at] = jnp.transpose(vals[at])

    pl.semaphore_wait(barrier, len(greeted))

    y_base, x_base, z_base, s_base = reserve(3), reserve(6), reserve(8), reserve(9)
    partner_side = (1, 3)
    for d in (1, 3, 2):
        remote(y_base + d - 1, cot, cots.at[y], y_dev[d])
    for j, d in enumerate((2, 6, 1, 7)):
        remote(z_base + j, feats, f_panel.at[own_r], z_dev[d])
    remote(s_base, feats, f_panel.at[own_r], sibling)

    for copy in local[:4]:
        copy.wait()
    mask = lists[3]
    ordered, counts = sort_tiles(lists[0], lists[1], lists[2], mask)
    meta_v[0:1, :] = ordered
    meta_v[1:2, 0:128] = counts
    meta_v[1:2, 128:384] = jnp.zeros((1, 256), I32)
    to_scalars = pltpu.make_async_copy(meta_v, meta_s, local_sems.at[13])
    to_scalars.start()

    def cot_arrived(d):
        arrived(y_base + d - 1, cots.at[(y + NY - d) % NY], y_dev[d])

    def f_slot(d, k):
        return 2 * ((z + NZ - d) % NZ) + k

    def make_products(hi, slot):
        total = dot(cots[2 * hi], weight[:, :256], ((1,), (1,)))
        total += dot(cots[2 * hi + 1], weight[:, 256:], ((1,), (1,)))
        panel[hi * NX + x] = total.astype(BF16).reshape(2, 128, 256)
        for j, d in enumerate((2, 1, 3)):
            remote(x_base + 3 * slot + j, panel.at[hi * NX + x], panel.at[hi * NX + x], device_at(z, core, (x + d) % NX, y))

    for copy in local[4:7]:
        copy.wait()
    cot_arrived(1)
    cot_arrived(3)
    make_products(y_hi, 0)

    ar_base = [reserve(1 + 7 + 7 + 7 + 8) for _ in range(2)]

    def share_send(a):
        remote(ar_base[a], share.at[a, pl.ds((1 - core) * 512, 512)], share_in.at[a], sibling)

    def share_cols(a):
        arrived(ar_base[a], share_in.at[a], sibling)
        total = share[a, pl.ds(core * 512, 512), :] + share_in[a]
        half_f[a] = total.reshape(8, 64, 128)
        half_b[a] = total.astype(BF16).reshape(8, 64, 128)
        for j in range(7):
            remote(ar_base[a] + 1 + j, half_b.at[a, col_to[j]], col_in.at[a, j], col_dev[j])

    def share_z(a):
        total = half_f[a, c_me]
        for j in range(7):
            arrived(ar_base[a] + 1 + j, col_in.at[a, j], col_dev[j])
            total += col_in[a, j].astype(F32)
        z_in[a, z] = total.astype(BF16)
        for d in (4, 3, 5, 2, 6, 1, 7):
            remote(ar_base[a] + 7 + d, z_in.at[a, z], z_in.at[a, z], z_dev[d])

    def share_back(a):
        for d in range(1, NZ):
            arrived(ar_base[a] + 7 + d, z_in.at[a, (z + NZ - d) % NZ], z_dev[d])
        total = z_in[a, 0].astype(F32)
        for d in range(1, NZ):
            total += z_in[a, d].astype(F32)
        mine = full.at[a, core, c_me]
        full[a, core, c_me] = total.astype(BF16)
        for j in range(7):
            remote(ar_base[a] + 15 + j, mine, mine, col_dev[j])
        remote(ar_base[a] + 22, mine, mine, sibling)

    def share_pass(a):
        for j in (6, 5, 3, 4, 2, 1, 0):
            block = full.at[a, core, col_from[j]]
            arrived(ar_base[a] + 15 + j, block, col_dev[j])
            remote(ar_base[a] + 23 + j, block, block, sibling)

    def share_end(a):
        arrived(ar_base[a] + 22, full.at[a, 1 - core, c_me], sibling)
        for j in range(7):
            arrived(ar_base[a] + 23 + j, full.at[a, 1 - core, col_from[j]], sibling)

    for j in range(2):
        w_part = dot(agg[...], cots[2 * y_hi + j], ((0,), (0,)))
        for i in range(2):
            at = 256 * (2 * j + i)
            share[0, at : at + 256, :] = w_part[:, 128 * i : 128 * i + 128]
    share_send(0)

    def f_pass(j, d):
        block = f_panel.at[f_slot(d, core)]
        arrived(z_base + j, block, z_dev[d])
        remote(s_base + 1 + j, block, block, sibling)

    turn_tiles(0)
    for side, d in enumerate((2, 6)):
        f_pass(side, d)
        block = f_panel.at[f_slot(d, core)]
        remote(z_base + 4 + side, block, block, z_dev[(1, 7)[side]])
        part = f_panel.at[f_slot(d, core), side]
        remote(z_base + 6 + side, part, part, z_dev[d])
    cot_arrived(2)
    make_products(1 - y_hi, 1)
    f_pass(2, 1)
    f_pass(3, 7)
    share_cols(0)
    for i in range(1, SLOTS // PART):
        turn_tiles(i)
    f_pass(4, 3)
    f_pass(5, 5)
    for side in range(2):
        part = f_panel.at[f_slot(4, core), side]
        arrived(z_base + 6 + side, part, z_dev[4])
        remote(s_base + 7 + side, part, part, sibling)
    for slot, hi in enumerate((y_hi, 1 - y_hi)):
        for j, d in enumerate((2, 1, 3)):
            arrived(
                x_base + 3 * slot + j, panel.at[hi * NX + (x + NX - d) % NX], device_at(z, core, (x + d) % NX, y)
            )
    arrived(s_base, f_panel.at[2 * z + 1 - core], sibling)
    for j, d in enumerate((2, 6, 1, 7, 3, 5)):
        arrived(s_base + 1 + j, f_panel.at[f_slot(d, 1 - core)], sibling)
    for side in range(2):
        arrived(s_base + 7 + side, f_panel.at[f_slot(4, 1 - core), side], sibling)
    share_z(0)
    local[7].wait()
    to_scalars.wait()

    @pl.loop(0, 16)
    def _(i):
        for h in range(2):
            f_wide[2 * i + h] = f_panel[i, h].astype(F32)

    @pl.loop(0, SLOTS // GROUP)
    def _(i):
        total = run[...]
        before = (meta_s[0, jnp.maximum(i * GROUP - 1, 0)] >> 4) & 31
        for g in range(GROUP):
            at = i * GROUP + g
            code = meta_s[0, at]
            r, c, q, k = code & 15, (code >> 4) & 31, (code >> 9) & 511, code >> 18
            moved = dot(vals[k], panel[r >> 1, r & 1], ((1,), (0,)))
            keep = (c == before).astype(F32)
            total = total * keep + moved * rv_wide[pl.ds(q, 1), :]
            prefix[at] = total.astype(BF16)
            parts[at] = jnp.sum((moved * f_wide[c]).reshape(16, 8, 256), axis=0)
            before = c
        run[...] = total

    n_base, m_base = reserve(8), reserve(14)
    needed = (4, 3, 5, 2, 6, 1, 7, 0)

    def column_sum(j):
        count = meta_s[1, j]
        before = meta_s[1, jnp.maximum(j - 1, 0)] * (j > 0).astype(I32)
        some = (count > before).astype(F32)
        return (prefix[jnp.maximum(count - 1, 0)].astype(F32) * some).astype(BF16)

    def send_sums(some):
        for i in some:
            for h in range(2):
                sums[i, h] = column_sum(4 * z_at[needed[i]] + 2 * (1 - core) + h)
            remote(n_base + i, sums.at[i], sib.at[i], sibling)

    send_sums(range(5))

    rel_sorted = (meta_v[0:1, :] // 512) % 512
    live = lax.broadcasted_iota(I32, (1, SLOTS), 1) < jnp.sum(mask, axis=1, keepdims=True)
    pick = jnp.where(
        (lax.broadcasted_iota(I32, (512, SLOTS), 0) == rel_sorted) & live, 1.0, 0.0
    ).astype(BF16)
    tile_rows = jnp.sum(parts[...], axis=1)
    high = tile_rows.astype(BF16)
    low = (tile_rows - high.astype(F32)).astype(BF16)
    rel_part = dot(pick, high, ((1,), (0,))) + dot(pick, low, ((1,), (0,)))
    share[1, 0:512, :] = rel_part[:, :128]
    share[1, 512:1024, :] = rel_part[:, 128:]
    share_send(1)
    send_sums(range(5, 8))

    def both(i, h):
        return column_sum(4 * z_at[needed[i]] + 2 * core + h).astype(F32) + sib[i, h].astype(F32)

    def ready(i):
        arrived(n_base + i, sib.at[i], sibling)

    def chain_sem(side, step, h):
        return m_base + 7 * side + (0 if step == 0 else 2 * step - 1 + h)

    def chain(side, step, h):
        total = both(0 if step == 0 else 2 * step - 1 + side, h)
        if step >= 2 or (step == 1 and h == side):
            arrived(chain_sem(side, step - 1, h), rx.at[side, step - 1, h], z_dev[(1, 7)[side]])
            total += rx[side, step - 1, h].astype(F32)
        tx[side, step, h] = total.astype(BF16)
        remote(chain_sem(side, step, h), tx.at[side, step, h], rx.at[side, step, h], z_dev[(1, 7)[side]])

    ready(0)
    for side in range(2):
        chain(side, 0, side)
    for side in range(2):
        ready(1 + side)
        chain(side, 1, 1 - side)
    share_cols(1)
    share_back(0)
    for side in range(2):
        chain(side, 1, side)
    for side in range(2):
        ready(3 + side)
        chain(side, 2, 1 - side)
    share_z(1)
    for side in range(2):
        chain(side, 2, side)
    for side in range(2):
        ready(5 + side)
        chain(side, 3, 1 - side)
    for side in range(2):
        chain(side, 3, side)
    share_pass(0)
    share_end(0)
    w_out[...] = full[0].reshape(1024, 128)
    share_back(1)
    ready(7)
    for h in range(2):
        total = both(7, h)
        for side in range(2):
            arrived(chain_sem(side, 3, h), rx.at[side, 3, h], z_dev[(1, 7)[side]])
            total += rx[side, 3, h].astype(F32)
        node_out[128 * h : 128 * h + 128, :] = total.astype(BF16)
    share_pass(1)
    share_end(1)
    rel_out[...] = full[1].reshape(1024, 128)
    for copy in pending:
        copy.wait_send()


def layer_call(*operands):
    hbm = pl.BlockSpec(memory_space=pltpu.HBM)
    vmem = pl.BlockSpec(memory_space=pltpu.VMEM)
    return pl.pallas_call(
        layer_kernel,
        out_shape=(
            jax.ShapeDtypeStruct((256, 256), BF16),
            jax.ShapeDtypeStruct((1024, 128), BF16),
            jax.ShapeDtypeStruct((1024, 128), BF16),
        ),
        in_specs=[hbm] * 10,
        out_specs=(vmem, vmem, vmem),
        scratch_shapes=[
            pltpu.VMEM((4, 1, SLOTS), I32),
            pltpu.VMEM((2, SLOTS), I32),
            pltpu.SMEM((2, SLOTS), I32),
            pltpu.VMEM((SLOTS, 128, 128), BF16),
            pltpu.VMEM((8, 2, 128, 256), BF16),
            pltpu.VMEM((16, 2, 128, 256), BF16),
            pltpu.VMEM((32, 128, 256), F32),
            pltpu.VMEM((512, 256), BF16),
            pltpu.VMEM((512, 256), F32),
            pltpu.VMEM((256, 256), BF16),
            pltpu.VMEM((256, 512), BF16),
            pltpu.VMEM((4, 256, 256), BF16),
            pltpu.VMEM((128, 256), F32),
            pltpu.VMEM((8, 128), F32),
            pltpu.VMEM((SLOTS, 8, 256), F32),
            pltpu.VMEM((SLOTS, 128, 256), BF16),
            pltpu.VMEM((8, 2, 128, 256), BF16),
            pltpu.VMEM((8, 2, 128, 256), BF16),
            pltpu.VMEM((2, 1024, 128), F32),
            pltpu.VMEM((2, 512, 128), F32),
            pltpu.VMEM((2, 8, 64, 128), F32),
            pltpu.VMEM((2, 8, 64, 128), BF16),
            pltpu.VMEM((2, 7, 64, 128), BF16),
            pltpu.VMEM((2, 8, 64, 128), BF16),
            pltpu.VMEM((2, 2, 8, 64, 128), BF16),
            pltpu.VMEM((2, 4, 2, 128, 256), BF16),
            pltpu.VMEM((2, 4, 2, 128, 256), BF16),
            pltpu.SemaphoreType.DMA((108,)),
            pltpu.SemaphoreType.DMA((108,)),
            pltpu.SemaphoreType.DMA((14,)),
        ],
        compiler_params=pltpu.CompilerParams(
            collective_id=0, has_side_effects=True, vmem_limit_bytes=62 * 2**20
        ),
        name="layer_backward",
    )(*operands)


def finish_kernel(scale, node, w, rel, node_out, w_out, rel_out):
    node_out[...] = node[...]
    for j in range(4):
        w_out[:, 128 * j : 128 * j + 128] = w[256 * j : 256 * j + 256, :].astype(F32) * scale
    for j in range(2):
        rel_out[:, 128 * j : 128 * j + 128] = rel[512 * j : 512 * j + 512, :].astype(F32)


def finish_call(scale, node, w, rel):
    vmem = pl.BlockSpec(memory_space=pltpu.VMEM)
    return pl.pallas_call(
        functools.partial(finish_kernel, scale),
        out_shape=(
            jax.ShapeDtypeStruct((256, 256), BF16),
            jax.ShapeDtypeStruct((256, 512), F32),
            jax.ShapeDtypeStruct((512, 256), F32),
        ),
        in_specs=[vmem] * 3,
        out_specs=(vmem,) * 3,
        name="finish",
    )(node, w, rel)


def on_device(
    node_feats, aggregated, cotangent, weight, relation_vecs, tile_vals, tile_row, tile_col, tile_rel, tile_mask
):
    nodes_total = node_feats.shape[0] * lax.axis_size("row") * lax.axis_size("col")
    node, w, rel = layer_call(
        node_feats.reshape(2, 128, 256),
        cotangent,
        aggregated,
        weight,
        relation_vecs,
        tile_vals.reshape(SLOTS, 128, 128),
        tile_row.reshape(1, SLOTS),
        tile_col.reshape(1, SLOTS),
        tile_rel.reshape(1, SLOTS),
        tile_mask.reshape(1, SLOTS),
    )
    return finish_call(nodes_total**-0.5, node, w, rel)


def solution(mesh):
    return jax.shard_map(
        on_device,
        mesh=mesh,
        in_specs=(
            P(("row", "col"), "feat"),
            P(("row", "col"), "feat"),
            P(("row", "col"), "feat"),
            P("feat", None),
            P(None, "feat"),
            P("row", "col", None, None, None),
            P("row", "col", None),
            P("row", "col", None),
            P("row", "col", None),
            P("row", "col", None),
        ),
        out_specs=(P(("row", "col"), "feat"), P("feat", None), P(None, "feat")),
        check_vma=False,
    )
```

```python
import functools

import jax
import jax.numpy as jnp
from jax import lax
from jax.experimental import pallas as pl
from jax.experimental.pallas import tpu as pltpu
from jax.sharding import PartitionSpec as P

MESH = pl.DeviceIdType.MESH
BF16 = jnp.bfloat16
F32 = jnp.float32
I32 = jnp.int32
NZ, NX, NY = 8, 4, 4
SLOTS = 384
GROUP = 48
PART = 96


def place():
    row, col, feat = lax.axis_index("row"), lax.axis_index("col"), lax.axis_index("feat")
    return row // 2, row % 2, col % NX, (col // NX) * 2 + feat


def device_at(z, core, x, y):
    return {"row": z * 2 + core, "col": (y // 2) * NX + x, "feat": y % 2}


def dot(a, b, contract):
    return lax.dot_general(a, b, ((contract[0], contract[1]), ((), ())), preferred_element_type=F32)


def columns_of(vector):
    return [
        jnp.transpose(jnp.broadcast_to(vector[:, 128 * b : 128 * b + 128], (128, 128))) for b in range(SLOTS // 128)
    ]


def over_rows(blocks):
    total = blocks[0]
    for block in blocks[1:]:
        total = total + block
    return jnp.sum(total, axis=0, keepdims=True)


def sort_tiles(row, col, rel, mask):
    slot = lax.broadcasted_iota(I32, (1, SLOTS), 1)
    key = col * 512 + slot + (1 - mask) * 32768
    packed = row + col * 16 + rel * 512 + slot * 262144
    key_columns = columns_of(key)
    lanes = lax.broadcasted_iota(I32, (128, 128), 1)
    ranks = [
        over_rows([(k < key[:, 128 * b : 128 * b + 128]).astype(I32) for k in key_columns])
        for b in range(SLOTS // 128)
    ]
    rank_columns = columns_of(jnp.concatenate(ranks, axis=1))
    packed_columns = columns_of(packed)
    ordered = [
        over_rows([jnp.where(r == lanes + 128 * b, p, 0) for r, p in zip(rank_columns, packed_columns)])
        for b in range(SLOTS // 128)
    ]
    counts = over_rows([(k < (lanes + 1) * 512).astype(I32) for k in key_columns])
    return jnp.concatenate(ordered, axis=1), counts


def layer_kernel(
    feats, cot, agg_h, weight_h, rv_h, vals_h, row_h, col_h, rel_h, mask_h,
    node_out, w_out, rel_out,
    lists, meta_v, meta_s, vals, panel, f_panel, f_wide, rv, rv_wide, agg, weight, cots,
    run, steps, parts, prefix, sums, sib,
    share, share_in, half_f, half_b, col_in, z_in, full,
    tx, rx, send_sems, recv_sems, local_sems,
):
    z, core, x, y = place()
    y_hi = y // 2
    c_me = y_hi * NX + x
    sibling = device_at(z, 1 - core, x, y)
    z_at = [(z + d) % NZ for d in range(NZ)]
    z_dev = [device_at(z_at[d], core, x, y) for d in range(NZ)]
    y_dev = [device_at(z, core, x, (y + d) % NY) for d in range(NY)]
    col_offsets = [(2, 2), (1, 2), (3, 2), (0, 2), (2, 0), (1, 0), (3, 0)]
    col_dev = [device_at(z, core, (x + dx) % NX, (y + dy) % NY) for dx, dy in col_offsets]
    col_to = [(((y + dy) % NY) // 2) * NX + (x + dx) % NX for dx, dy in col_offsets]
    col_from = [(((y + dy) % NY) // 2) * NX + (x + NX - dx) % NX for dx, dy in col_offsets]
    pending = []
    taken = [0]

    def reserve(n):
        taken[0] += n
        return taken[0] - n

    def remote(i, src, dst, device):
        copy = pltpu.make_async_remote_copy(
            src_ref=src, dst_ref=dst, send_sem=send_sems.at[i], recv_sem=recv_sems.at[i],
            device_id=device, device_id_type=MESH,
        )
        copy.start()
        pending.append(copy)

    def arrived(i, ref, device):
        pltpu.make_async_remote_copy(
            src_ref=ref, dst_ref=ref, send_sem=send_sems.at[i], recv_sem=recv_sems.at[i],
            device_id=device, device_id_type=MESH,
        ).wait_recv()

    own_r = 2 * z + core
    local = [
        pltpu.make_async_copy(src, dst, local_sems.at[i])
        for i, (src, dst) in enumerate(
            (
                (row_h, lists.at[0]), (col_h, lists.at[1]), (rel_h, lists.at[2]), (mask_h, lists.at[3]),
                (cot, cots.at[y]), (weight_h, weight), (agg_h, agg), (feats, f_panel.at[own_r]),
                (rv_h, rv),
                *((vals_h.at[pl.ds(PART * i, PART)], vals.at[pl.ds(PART * i, PART)]) for i in range(SLOTS // PART)),
            )
        )
    ]
    for copy in local:
        copy.start()

    barrier = pltpu.get_barrier_semaphore()
    greeted = [sibling, *z_dev[1:], *col_dev, y_dev[1], y_dev[3]]
    for device in greeted:
        pl.semaphore_signal(barrier, inc=1, device_id=device, device_id_type=MESH)
    run[...] = jnp.zeros_like(run)
    local[8].wait()
    rv_wide[...] = rv[...].astype(F32)

    def turn_tiles(i):
        local[9 + i].wait()

        @pl.loop(0, PART // 16)
        def _(j):
            for g in range(16):
                at = i * PART + j * 16 + g
                vals[at] = jnp.transpose(vals[at])

    pl.semaphore_wait(barrier, len(greeted))

    y_base, x_base, z_base, s_base = reserve(3), reserve(6), reserve(8), reserve(9)
    partner_side = (1, 3)
    for d in (1, 3, 2):
        remote(y_base + d - 1, cot, cots.at[y], y_dev[d])
    for j, d in enumerate((2, 6, 1, 7)):
        remote(z_base + j, feats, f_panel.at[own_r], z_dev[d])
    remote(s_base, feats, f_panel.at[own_r], sibling)

    for copy in local[:4]:
        copy.wait()
    mask = lists[3]
    ordered, counts = sort_tiles(lists[0], lists[1], lists[2], mask)
    meta_v[0:1, :] = ordered
    meta_v[1:2, 0:128] = counts
    meta_v[1:2, 128:384] = jnp.zeros((1, 256), I32)
    to_scalars = pltpu.make_async_copy(meta_v, meta_s, local_sems.at[13])
    to_scalars.start()

    def cot_arrived(d):
        arrived(y_base + d - 1, cots.at[(y + NY - d) % NY], y_dev[d])

    def f_slot(d, k):
        return 2 * ((z + NZ - d) % NZ) + k

    def make_products(hi, slot):
        total = dot(cots[2 * hi], weight[:, :256], ((1,), (1,)))
        total += dot(cots[2 * hi + 1], weight[:, 256:], ((1,), (1,)))
        panel[hi * NX + x] = total.astype(BF16).reshape(2, 128, 256)
        for j, d in enumerate((2, 1, 3)):
            remote(x_base + 3 * slot + j, panel.at[hi * NX + x], panel.at[hi * NX + x], device_at(z, core, (x + d) % NX, y))

    for copy in local[4:7]:
        copy.wait()
    cot_arrived(1)
    cot_arrived(3)
    make_products(y_hi, 0)

    ar_base = [reserve(1 + 7 + 7 + 7 + 8) for _ in range(2)]

    def share_send(a):
        remote(ar_base[a], share.at[a, pl.ds((1 - core) * 512, 512)], share_in.at[a], sibling)

    def share_cols(a):
        arrived(ar_base[a], share_in.at[a], sibling)
        total = share[a, pl.ds(core * 512, 512), :] + share_in[a]
        half_f[a] = total.reshape(8, 64, 128)
        half_b[a] = total.astype(BF16).reshape(8, 64, 128)
        for j in range(7):
            remote(ar_base[a] + 1 + j, half_b.at[a, col_to[j]], col_in.at[a, j], col_dev[j])

    def share_z(a):
        total = half_f[a, c_me]
        for j in range(7):
            arrived(ar_base[a] + 1 + j, col_in.at[a, j], col_dev[j])
            total += col_in[a, j].astype(F32)
        z_in[a, z] = total.astype(BF16)
        for d in (4, 3, 5, 2, 6, 1, 7):
            remote(ar_base[a] + 7 + d, z_in.at[a, z], z_in.at[a, z], z_dev[d])

    def share_back(a):
        for d in range(1, NZ):
            arrived(ar_base[a] + 7 + d, z_in.at[a, (z + NZ - d) % NZ], z_dev[d])
        total = z_in[a, 0].astype(F32)
        for d in range(1, NZ):
            total += z_in[a, d].astype(F32)
        mine = full.at[a, core, c_me]
        full[a, core, c_me] = total.astype(BF16)
        for j in range(7):
            remote(ar_base[a] + 15 + j, mine, mine, col_dev[j])
        remote(ar_base[a] + 22, mine, mine, sibling)

    def share_pass(a):
        for j in (6, 5, 3, 4, 2, 1, 0):
            block = full.at[a, core, col_from[j]]
            arrived(ar_base[a] + 15 + j, block, col_dev[j])
            remote(ar_base[a] + 23 + j, block, block, sibling)

    def share_end(a):
        arrived(ar_base[a] + 22, full.at[a, 1 - core, c_me], sibling)
        for j in range(7):
            arrived(ar_base[a] + 23 + j, full.at[a, 1 - core, col_from[j]], sibling)

    for j in range(2):
        w_part = dot(agg[...], cots[2 * y_hi + j], ((0,), (0,)))
        for i in range(2):
            at = 256 * (2 * j + i)
            share[0, at : at + 256, :] = w_part[:, 128 * i : 128 * i + 128]
    share_send(0)

    def f_pass(j, d):
        block = f_panel.at[f_slot(d, core)]
        arrived(z_base + j, block, z_dev[d])
        remote(s_base + 1 + j, block, block, sibling)

    for side, d in enumerate((2, 6)):
        f_pass(side, d)
        block = f_panel.at[f_slot(d, core)]
        remote(z_base + 4 + side, block, block, z_dev[(1, 7)[side]])
        part = f_panel.at[f_slot(d, core), side]
        remote(z_base + 6 + side, part, part, z_dev[d])
    cot_arrived(2)
    make_products(1 - y_hi, 1)
    f_pass(2, 1)
    f_pass(3, 7)
    share_cols(0)
    for i in range(SLOTS // PART):
        turn_tiles(i)
    f_pass(4, 3)
    f_pass(5, 5)
    for side in range(2):
        part = f_panel.at[f_slot(4, core), side]
        arrived(z_base + 6 + side, part, z_dev[4])
        remote(s_base + 7 + side, part, part, sibling)
    for slot, hi in enumerate((y_hi, 1 - y_hi)):
        for j, d in enumerate((2, 1, 3)):
            arrived(
                x_base + 3 * slot + j, panel.at[hi * NX + (x + NX - d) % NX], device_at(z, core, (x + d) % NX, y)
            )
    arrived(s_base, f_panel.at[2 * z + 1 - core], sibling)
    for j, d in enumerate((2, 6, 1, 7, 3, 5)):
        arrived(s_base + 1 + j, f_panel.at[f_slot(d, 1 - core)], sibling)
    for side in range(2):
        arrived(s_base + 7 + side, f_panel.at[f_slot(4, 1 - core), side], sibling)
    share_z(0)
    local[7].wait()
    to_scalars.wait()

    @pl.loop(0, 16)
    def _(i):
        for h in range(2):
            f_wide[2 * i + h] = f_panel[i, h].astype(F32)

    @pl.loop(0, SLOTS // GROUP)
    def _(i):
        total = run[...]
        before = (meta_s[0, jnp.maximum(i * GROUP - 1, 0)] >> 4) & 31
        for g in range(GROUP):
            at = i * GROUP + g
            code = meta_s[0, at]
            r, c, q, k = code & 15, (code >> 4) & 31, (code >> 9) & 511, code >> 18
            moved = dot(vals[k], panel[r >> 1, r & 1], ((1,), (0,)))
            keep = (c == before).astype(F32)
            total = total * keep + moved * rv_wide[pl.ds(q, 1), :]
            prefix[at] = total.astype(BF16)
            parts[at] = jnp.sum((moved * f_wide[c]).reshape(16, 8, 256), axis=0)
            before = c
        run[...] = total

    n_base, m_base = reserve(8), reserve(14)
    needed = (4, 3, 5, 2, 6, 1, 7, 0)

    def column_sum(j):
        count = meta_s[1, j]
        before = meta_s[1, jnp.maximum(j - 1, 0)] * (j > 0).astype(I32)
        some = (count > before).astype(F32)
        return (prefix[jnp.maximum(count - 1, 0)].astype(F32) * some).astype(BF16)

    def send_sums(some):
        for i in some:
            for h in range(2):
                sums[i, h] = column_sum(4 * z_at[needed[i]] + 2 * (1 - core) + h)
            remote(n_base + i, sums.at[i], sib.at[i], sibling)

    send_sums(range(5))

    rel_sorted = (meta_v[0:1, :] // 512) % 512
    live = lax.broadcasted_iota(I32, (1, SLOTS), 1) < jnp.sum(mask, axis=1, keepdims=True)
    pick = jnp.where(
        (lax.broadcasted_iota(I32, (512, SLOTS), 0) == rel_sorted) & live, 1.0, 0.0
    ).astype(BF16)
    tile_rows = jnp.sum(parts[...], axis=1)
    high = tile_rows.astype(BF16)
    low = (tile_rows - high.astype(F32)).astype(BF16)
    rel_part = dot(pick, high, ((1,), (0,))) + dot(pick, low, ((1,), (0,)))
    share[1, 0:512, :] = rel_part[:, :128]
    share[1, 512:1024, :] = rel_part[:, 128:]
    share_send(1)
    send_sums(range(5, 8))

    def both(i, h):
        return column_sum(4 * z_at[needed[i]] + 2 * core + h).astype(F32) + sib[i, h].astype(F32)

    def ready(i):
        arrived(n_base + i, sib.at[i], sibling)

    def chain_sem(side, step, h):
        return m_base + 7 * side + (0 if step == 0 else 2 * step - 1 + h)

    def chain(side, step, h):
        total = both(0 if step == 0 else 2 * step - 1 + side, h)
        if step >= 2 or (step == 1 and h == side):
            arrived(chain_sem(side, step - 1, h), rx.at[side, step - 1, h], z_dev[(1, 7)[side]])
            total += rx[side, step - 1, h].astype(F32)
        tx[side, step, h] = total.astype(BF16)
        remote(chain_sem(side, step, h), tx.at[side, step, h], rx.at[side, step, h], z_dev[(1, 7)[side]])

    ready(0)
    for side in range(2):
        chain(side, 0, side)
    for side in range(2):
        ready(1 + side)
        chain(side, 1, 1 - side)
    share_cols(1)
    share_back(0)
    for side in range(2):
        chain(side, 1, side)
    for side in range(2):
        ready(3 + side)
        chain(side, 2, 1 - side)
    share_z(1)
    for side in range(2):
        chain(side, 2, side)
    for side in range(2):
        ready(5 + side)
        chain(side, 3, 1 - side)
    for side in range(2):
        chain(side, 3, side)
    share_pass(0)
    share_end(0)
    w_out[...] = full[0].reshape(1024, 128)
    share_back(1)
    ready(7)
    for h in range(2):
        total = both(7, h)
        for side in range(2):
            arrived(chain_sem(side, 3, h), rx.at[side, 3, h], z_dev[(1, 7)[side]])
            total += rx[side, 3, h].astype(F32)
        node_out[128 * h : 128 * h + 128, :] = total.astype(BF16)
    share_pass(1)
    share_end(1)
    rel_out[...] = full[1].reshape(1024, 128)
    for copy in pending:
        copy.wait_send()


def layer_call(*operands):
    hbm = pl.BlockSpec(memory_space=pltpu.HBM)
    vmem = pl.BlockSpec(memory_space=pltpu.VMEM)
    return pl.pallas_call(
        layer_kernel,
        out_shape=(
            jax.ShapeDtypeStruct((256, 256), BF16),
            jax.ShapeDtypeStruct((1024, 128), BF16),
            jax.ShapeDtypeStruct((1024, 128), BF16),
        ),
        in_specs=[hbm] * 10,
        out_specs=(vmem, vmem, vmem),
        scratch_shapes=[
            pltpu.VMEM((4, 1, SLOTS), I32),
            pltpu.VMEM((2, SLOTS), I32),
            pltpu.SMEM((2, SLOTS), I32),
            pltpu.VMEM((SLOTS, 128, 128), BF16),
            pltpu.VMEM((8, 2, 128, 256), BF16),
            pltpu.VMEM((16, 2, 128, 256), BF16),
            pltpu.VMEM((32, 128, 256), F32),
            pltpu.VMEM((512, 256), BF16),
            pltpu.VMEM((512, 256), F32),
            pltpu.VMEM((256, 256), BF16),
            pltpu.VMEM((256, 512), BF16),
            pltpu.VMEM((4, 256, 256), BF16),
            pltpu.VMEM((128, 256), F32),
            pltpu.VMEM((8, 128), F32),
            pltpu.VMEM((SLOTS, 8, 256), F32),
            pltpu.VMEM((SLOTS, 128, 256), BF16),
            pltpu.VMEM((8, 2, 128, 256), BF16),
            pltpu.VMEM((8, 2, 128, 256), BF16),
            pltpu.VMEM((2, 1024, 128), F32),
            pltpu.VMEM((2, 512, 128), F32),
            pltpu.VMEM((2, 8, 64, 128), F32),
            pltpu.VMEM((2, 8, 64, 128), BF16),
            pltpu.VMEM((2, 7, 64, 128), BF16),
            pltpu.VMEM((2, 8, 64, 128), BF16),
            pltpu.VMEM((2, 2, 8, 64, 128), BF16),
            pltpu.VMEM((2, 4, 2, 128, 256), BF16),
            pltpu.VMEM((2, 4, 2, 128, 256), BF16),
            pltpu.SemaphoreType.DMA((108,)),
            pltpu.SemaphoreType.DMA((108,)),
            pltpu.SemaphoreType.DMA((14,)),
        ],
        compiler_params=pltpu.CompilerParams(
            collective_id=0, has_side_effects=True, vmem_limit_bytes=62 * 2**20
        ),
        name="layer_backward",
    )(*operands)


def finish_kernel(scale, node, w, rel, node_out, w_out, rel_out):
    node_out[...] = node[...]
    for j in range(4):
        w_out[:, 128 * j : 128 * j + 128] = w[256 * j : 256 * j + 256, :].astype(F32) * scale
    for j in range(2):
        rel_out[:, 128 * j : 128 * j + 128] = rel[512 * j : 512 * j + 512, :].astype(F32)


def finish_call(scale, node, w, rel):
    vmem = pl.BlockSpec(memory_space=pltpu.VMEM)
    return pl.pallas_call(
        functools.partial(finish_kernel, scale),
        out_shape=(
            jax.ShapeDtypeStruct((256, 256), BF16),
            jax.ShapeDtypeStruct((256, 512), F32),
            jax.ShapeDtypeStruct((512, 256), F32),
        ),
        in_specs=[vmem] * 3,
        out_specs=(vmem,) * 3,
        name="finish",
    )(node, w, rel)


def on_device(
    node_feats, aggregated, cotangent, weight, relation_vecs, tile_vals, tile_row, tile_col, tile_rel, tile_mask
):
    nodes_total = node_feats.shape[0] * lax.axis_size("row") * lax.axis_size("col")
    node, w, rel = layer_call(
        node_feats.reshape(2, 128, 256),
        cotangent,
        aggregated,
        weight,
        relation_vecs,
        tile_vals.reshape(SLOTS, 128, 128),
        tile_row.reshape(1, SLOTS),
        tile_col.reshape(1, SLOTS),
        tile_rel.reshape(1, SLOTS),
        tile_mask.reshape(1, SLOTS),
    )
    return finish_call(nodes_total**-0.5, node, w, rel)


def solution(mesh):
    return jax.shard_map(
        on_device,
        mesh=mesh,
        in_specs=(
            P(("row", "col"), "feat"),
            P(("row", "col"), "feat"),
            P(("row", "col"), "feat"),
            P("feat", None),
            P(None, "feat"),
            P("row", "col", None, None, None),
            P("row", "col", None),
            P("row", "col", None),
            P("row", "col", None),
            P("row", "col", None),
        ),
        out_specs=(P(("row", "col"), "feat"), P("feat", None), P(None, "feat")),
        check_vma=False,
    )
```
